256 devices in a mesh: lat: 16 (over z, y_lo), mp: 16 (over y_hi, x, core).
Axes of the slice: x: 4, y: 4 (y_hi: 2, y_lo: 2; y = y_hi * 2 + y_lo), z: 8, core: 2. Of those that a mesh axis runs over, the one named last changes fastest.
Arguments:
- tokens: bfloat16 [32768, 1024], P(('lat', 'mp')), may hold values from -20 to 20
- gain: float32 [1024], replicated, may hold values from 0.1 to 1.9
- qkv_weight: bfloat16 [16, 192, 1024], P('mp'), may hold values from -2 to 2
- out_weight: bfloat16 [16, 64, 1024], P('mp'), may hold values from -1 to 1
- row_cells: int32 [128], replicated, may hold values from 32 to 256, as said below
- upstream: bfloat16 [32768, 1024], P(('lat', 'mp')), may hold values from -6 to 6
Outputs:
- update: bfloat16 [32768, 1024], P(('lat', 'mp'))
- grad_input: bfloat16 [32768, 1024], P(('lat', 'mp'))
- grad_qkv: float32 [16, 192, 1024], P('mp')
- grad_out: float32 [16, 64, 1024], P('mp')
The draws below stay inside these ranges and needn't reach their ends.
Inputs may be any that keep to these rules, and one draw needn't show every extreme that they name: `row_cells`: A row's live cells are its first ones; rows at the equator hold all 256, rows at the poles 256 // 8.
All inputs are finite; a program needn't handle non-finite values.
Results may differ from the reference program's by a relative error of at most 0.0085.
The reference program's roundings to bfloat16 on the way count: a program that leaves them out, or rounds other values in their place, can miss the bound.
Values may be sent and summed in bfloat16 or wider, within the bound.
A program may use at most 64 MiB of HBM per device.

```python
import math
import jax
import jax.numpy as jnp
from jax import lax

WIDTH = 1024
HEAD_COUNT = 16
HEAD_WIDTH = 64
LONGITUDES = 256
LATITUDES = 128
TOKEN_COUNT = 32768


def draw_tokens(key, part):
    key = jax.random.fold_in(key, 11)
    base_key = jax.random.fold_in(key, 0)
    draws = jnp.clip(jax.random.normal(base_key, (TOKEN_COUNT, WIDTH), jnp.float32), -6.0, 6.0)
    return draws.astype(jnp.bfloat16)


def draw_qkv_weight(key, part):
    key = jax.random.fold_in(key, 12)
    query_key, keys_key, value_key = jax.random.split(key, 3)
    spread = 1.0 / math.sqrt(WIDTH)
    array_shape = (HEAD_COUNT, HEAD_WIDTH, WIDTH)
    queries = jnp.clip(jax.random.normal(query_key, array_shape, jnp.float32), -4.0, 4.0) * spread
    keys_part = jnp.clip(jax.random.normal(keys_key, array_shape, jnp.float32), -4.0, 4.0) * spread
    values = jnp.clip(jax.random.normal(value_key, array_shape, jnp.float32), -4.0, 4.0) * spread
    return jnp.concatenate([queries, keys_part, values], axis=1).astype(jnp.bfloat16)


def draw_out_weight(key, part):
    key = jax.random.fold_in(key, 13)
    base_key, order_key = jax.random.split(key)
    order = jax.random.permutation(order_key, HEAD_COUNT).astype(jnp.float32)
    exponent = order / max(1, HEAD_COUNT - 1) - 0.5
    head_scale = jnp.exp(exponent * math.log(16.0))
    head_scale = head_scale / jnp.sqrt(jnp.mean(head_scale * head_scale))
    draws = jnp.clip(jax.random.normal(base_key, (HEAD_COUNT, HEAD_WIDTH, WIDTH), jnp.float32), -4.0, 4.0)
    draws = draws * (1.0 / math.sqrt(WIDTH)) * head_scale[:, None, None]
    return draws.astype(jnp.bfloat16)


def draw_row_cells(key, part):
    key = jax.random.fold_in(key, 14)
    row_index = jnp.arange(LATITUDES, dtype=jnp.int32)
    distance = jnp.abs(2 * row_index - (LATITUDES - 1))
    jitter = jax.random.randint(key, (LATITUDES,), 0, LONGITUDES // 16 + 1, dtype=jnp.int32)
    live_cells = LONGITUDES + LONGITUDES // 16 - LONGITUDES * distance * distance // (LATITUDES * LATITUDES) - jitter
    return jnp.clip(live_cells, LONGITUDES // 8, LONGITUDES).astype(jnp.int32)


def block_levels(stream_key, shape, shards, least, largest):
    def one(axis_at, blocks):
        heights = jax.random.uniform(jax.random.fold_in(jax.random.fold_in(stream_key, 6), axis_at), (blocks,), jnp.float32, least / len(shards), largest / len(shards))
        return jnp.repeat(jnp.exp(heights), shape[axis_at] // blocks).reshape((-1,) + (1,) * (len(shape) - axis_at - 1))

    loudness = one(*shards[0])
    for cut in shards[1:]:
        loudness = loudness * one(*cut)
    return loudness


def normal_values(own_key, shape, scale, reach, shards=(), kind=jnp.bfloat16):
    result = scale * jax.random.normal(own_key, shape, jnp.float32)
    if shards:
        result = result * block_levels(own_key, shape, shards, -0.22, 0.18)
    return jnp.clip(result, -reach, reach).astype(kind)


def setup_inputs(seed: int = 0) -> dict:
    seeds = jax.random.split(jax.random.key(seed), 7)
    return {
        "tokens": draw_tokens(jax.random.fold_in(seeds[6], 71), 0),
        "gain": jnp.clip(1.0 + 0.18 * jax.random.normal(seeds[1], (WIDTH,), jnp.float32), 0.1, 1.9),
        "qkv_weight": draw_qkv_weight(jax.random.fold_in(seeds[6], 71), 0),
        "out_weight": draw_out_weight(jax.random.fold_in(seeds[6], 71), 0),
        "row_cells": draw_row_cells(jax.random.fold_in(seeds[6], 71), 0),
        "upstream": normal_values(seeds[5], (TOKEN_COUNT, WIDTH), 1.0, 6.0, ((0, 256),)),
    }


def rounded(array):
    return lax.optimization_barrier(array.astype(jnp.bfloat16))

def tile_mask(row_start, col_start, cells_pad, col_tile, key_cols):
    query_rows = jnp.arange(4, dtype=jnp.int32)
    key_rows = jnp.arange(16, dtype=jnp.int32)
    query_cols = col_start + jnp.arange(col_tile, dtype=jnp.int32)
    key_index = (col_start - 8 + jnp.arange(key_cols, dtype=jnp.int32)) % LONGITUDES
    query_cells = lax.dynamic_slice_in_dim(cells_pad, row_start + 6, 4)
    key_cells = lax.dynamic_slice_in_dim(cells_pad, row_start, 16)
    query_live = query_cols[None, :] < query_cells[:, None]
    key_live = key_index[None, :] < key_cells[:, None]
    row_near = jnp.abs(key_rows[None, :] - 6 - query_rows[:, None]) <= 6
    offset = (key_index[None, :] - query_cols[:, None]) % LONGITUDES
    col_near = (offset <= 6) | (offset >= LONGITUDES - 6)
    allowed = query_live[:, :, None, None] & key_live[None, None, :, :] & row_near[:, None, :, None] & col_near[None, :, None, :]
    return (allowed.reshape(4 * col_tile, 16 * key_cols), query_live.reshape(4 * col_tile), key_index)

def tile_probs(queries, keys_tile, allowed, query_live, score_scale):
    scores = jnp.einsum('qhd,khd->hqk', queries.astype(jnp.float32), keys_tile.astype(jnp.float32)) * score_scale
    masked = jnp.where(allowed[None], scores, -1e+30)
    highest = lax.optimization_barrier(jnp.max(masked, axis=2, keepdims=True))
    terms = jnp.where(allowed[None], jnp.exp(masked - highest), 0.0)
    total = lax.optimization_barrier(jnp.sum(terms, axis=2, keepdims=True)) + (1.0 - query_live.astype(jnp.float32))[None, :, None]
    return terms / total

def assemble(tiles, row_total, col_tile, heads, width):
    layout = tiles.reshape(row_total // 4, LONGITUDES // col_tile, 4, col_tile, heads, width)
    return layout.transpose(0, 2, 1, 3, 4, 5).reshape(row_total * LONGITUDES, heads * width)

def reference(tokens, gain, qkv_weight, out_weight, row_cells, upstream):
    score_scale = 1.0 / math.sqrt(HEAD_WIDTH)
    grad_scale = 4.0 / math.sqrt(TOKEN_COUNT)
    col_tile = min(128, LONGITUDES)
    key_cols = min(LONGITUDES, col_tile + 16)
    col_tiles = LONGITUDES // col_tile
    tile_count = LATITUDES // 4 * col_tiles
    zero_index = jnp.zeros((), jnp.int32)
    features = tokens.astype(jnp.float32)
    inverse = lax.rsqrt(lax.optimization_barrier(jnp.mean(features * features, axis=1, keepdims=True)) + 1e-06)
    normed = rounded(features * inverse * gain[None, :])
    qkv_flat_weight = qkv_weight.reshape(HEAD_COUNT * 3 * HEAD_WIDTH, WIDTH)
    qkv_flat = rounded(lax.dot_general(normed, qkv_flat_weight, (((1,), (1,)), ((), ())), preferred_element_type=jnp.float32))
    qkv_grid = qkv_flat.reshape(LATITUDES, LONGITUDES, HEAD_COUNT, 3 * HEAD_WIDTH)
    queries_all = qkv_grid[..., :HEAD_WIDTH]
    keyval_pad = jnp.pad(qkv_grid[..., HEAD_WIDTH:], ((6, 6), (0, 0), (0, 0), (0, 0)))
    cells_pad = jnp.pad(row_cells, (6, 6))

    def tile_anchor(tile_index):
        return (tile_index // col_tiles * 4, tile_index % col_tiles * col_tile)

    def tile_inputs(tile_index):
        row_start, col_start = tile_anchor(tile_index)
        allowed, query_live, key_index = tile_mask(row_start, col_start, cells_pad, col_tile, key_cols)
        queries = lax.dynamic_slice(queries_all, (row_start, col_start, zero_index, zero_index), (4, col_tile, HEAD_COUNT, HEAD_WIDTH)).reshape(4 * col_tile, HEAD_COUNT, HEAD_WIDTH)
        key_block = jnp.take(lax.dynamic_slice_in_dim(keyval_pad, row_start, 16, 0), key_index, axis=1)
        key_block = key_block.reshape(16 * key_cols, HEAD_COUNT, 2 * HEAD_WIDTH)
        return (allowed, query_live, key_index, queries, key_block)

    def forward_tile(tile_index):
        allowed, query_live, key_index, queries, key_block = tile_inputs(tile_index)
        probabilities = tile_probs(queries, key_block[..., :HEAD_WIDTH], allowed, query_live, score_scale)
        weights = rounded(probabilities).astype(jnp.float32)
        return rounded(jnp.einsum('hqk,khd->qhd', weights, key_block[..., HEAD_WIDTH:].astype(jnp.float32)))
    tile_ids = jnp.arange(tile_count, dtype=jnp.int32)
    heads_out = assemble(lax.map(forward_tile, tile_ids), LATITUDES, col_tile, HEAD_COUNT, HEAD_WIDTH)
    out_flat = out_weight.reshape(HEAD_COUNT * HEAD_WIDTH, WIDTH)
    update = jnp.dot(heads_out, out_flat, preferred_element_type=jnp.float32).astype(jnp.bfloat16)
    grad_heads = rounded(jnp.dot(upstream, out_flat.T, preferred_element_type=jnp.float32))
    grad_out = jnp.dot(heads_out.T, upstream, preferred_element_type=jnp.float32) * grad_scale
    grad_out = grad_out.reshape(HEAD_COUNT, HEAD_WIDTH, WIDTH)
    grad_grid = grad_heads.reshape(LATITUDES, LONGITUDES, HEAD_COUNT, HEAD_WIDTH)

    def backward_tile(key_accum, tile_index):
        allowed, query_live, key_index, queries, key_block = tile_inputs(tile_index)
        row_start, col_start = tile_anchor(tile_index)
        grad_tile = lax.dynamic_slice(grad_grid, (row_start, col_start, zero_index, zero_index), (4, col_tile, HEAD_COUNT, HEAD_WIDTH)).reshape(4 * col_tile, HEAD_COUNT, HEAD_WIDTH)
        grad_tile = grad_tile.astype(jnp.float32)
        keys_tile = key_block[..., :HEAD_WIDTH].astype(jnp.float32)
        values_tile = key_block[..., HEAD_WIDTH:].astype(jnp.float32)
        probabilities = tile_probs(queries, keys_tile, allowed, query_live, score_scale)
        weights = rounded(probabilities).astype(jnp.float32)
        grad_probs = jnp.einsum('qhd,khd->hqk', grad_tile, values_tile)
        row_delta = lax.optimization_barrier(jnp.sum(probabilities * grad_probs, axis=2, keepdims=True))
        grad_scores = rounded(probabilities * (grad_probs - row_delta)).astype(jnp.float32)
        grad_query = rounded(jnp.einsum('hqk,khd->qhd', grad_scores, keys_tile) * score_scale)
        grad_key = jnp.einsum('hqk,qhd->khd', grad_scores, queries.astype(jnp.float32)) * score_scale
        grad_value = jnp.einsum('hqk,qhd->khd', weights, grad_tile)
        key_grads = jnp.concatenate([grad_key, grad_value], axis=2).reshape(16, key_cols, HEAD_COUNT, 2 * HEAD_WIDTH)
        rows_hit = row_start + jnp.arange(16, dtype=jnp.int32)
        key_accum = key_accum.at[rows_hit[:, None], key_index[None, :]].add(key_grads)
        return (key_accum, grad_query)
    accum_start = jnp.zeros((LATITUDES + 12, LONGITUDES, HEAD_COUNT, 2 * HEAD_WIDTH), jnp.float32)
    key_accum, query_tiles = lax.scan(backward_tile, accum_start, tile_ids)
    grad_query_all = assemble(query_tiles, LATITUDES, col_tile, HEAD_COUNT, HEAD_WIDTH)
    grad_query_all = grad_query_all.reshape(TOKEN_COUNT, HEAD_COUNT, HEAD_WIDTH)
    grad_keyval = key_accum[6:LATITUDES + 6].astype(jnp.bfloat16).reshape(TOKEN_COUNT, HEAD_COUNT, 2 * HEAD_WIDTH)
    grad_proj = jnp.concatenate([grad_query_all, grad_keyval], axis=2).reshape(TOKEN_COUNT, HEAD_COUNT * 3 * HEAD_WIDTH)
    grad_qkv = lax.dot_general(grad_proj, normed, (((0,), (0,)), ((), ())), preferred_element_type=jnp.float32) * grad_scale
    grad_qkv = grad_qkv.reshape(HEAD_COUNT, 3 * HEAD_WIDTH, WIDTH)
    grad_normed = jnp.dot(grad_proj, qkv_flat_weight, preferred_element_type=jnp.float32)
    centred = features * inverse
    scaled = gain[None, :] * grad_normed
    grad_input = inverse * (scaled - centred * lax.optimization_barrier(jnp.mean(scaled * centred, axis=1, keepdims=True)))
    return (update, grad_input.astype(jnp.bfloat16), grad_qkv, grad_out)
```

```python
import math

import jax
import jax.numpy as jnp
from jax import lax
from jax.experimental import pallas as pl
from jax.experimental.pallas import tpu as pltpu
from jax.sharding import PartitionSpec as P

WIDTH = 1024
HEAD_WIDTH = 64
LONGITUDES = 256
BAND_ROWS = 8
REACH = 6
KEY_ROWS = BAND_ROWS + 2 * REACH
TILE = 16
WINDOW = 2 * TILE
TILES = LONGITUDES // TILE
KEY_COLS = LONGITUDES + TILE
QUERY_COLS = LONGITUDES + TILE // 2
NEVER = -1e30
VMEM = pltpu.VMEM


def passed_along(x, axis, by):
    length = lax.axis_size(axis)
    pairs = [(i, i + by) for i in range(length) if 0 <= i + by < length]
    return lax.ppermute(x, axis, pairs)


def key_features(cells):
    shape = (KEY_ROWS, KEY_COLS, 128)
    row = lax.broadcasted_iota(jnp.int32, shape, 0)
    col = lax.broadcasted_iota(jnp.int32, shape, 1)
    lane = lax.broadcasted_iota(jnp.int32, shape, 2)
    live = col % LONGITUDES < cells[:, None, None]
    near_row = (row >= lane - 8) & (row <= lane - 8 + 2 * REACH)
    apart = (col - lane) % 32
    near_col = (apart <= REACH) | (apart >= 32 - REACH)
    barred = (
        ((lane == 0) & ~live)
        | ((lane >= 8) & (lane < 16) & ~near_row)
        | ((lane >= 32) & (lane < 64) & ~near_col)
    )
    return jnp.where(barred, NEVER, 0.0).astype(jnp.bfloat16)


def query_features():
    shape = (2, BAND_ROWS, TILE, 128)
    tile, row, col, lane = (lax.broadcasted_iota(jnp.int32, shape, d) for d in range(4))
    picked = (
        (lane == 0)
        | (lane == 8 + row)
        | (lane == 32 + (TILE * tile + TILE // 2 + col) % 32)
    )
    return picked.astype(jnp.bfloat16).reshape(2, BAND_ROWS * TILE, 128)


def live_queries(cells):
    shape = (TILES, 1, BAND_ROWS, TILE)
    tile, _, _, col = (lax.broadcasted_iota(jnp.int32, shape, d) for d in range(4))
    at = (TILE * tile + TILE // 2 + col) % LONGITUDES
    live = at < cells[REACH : REACH + BAND_ROWS][None, None, :, None]
    return live.astype(jnp.float32).reshape(TILES, 1, BAND_ROWS * TILE)


def attention_tile(i, kv_ref, feat_ref, q_ref, g_ref, pick_ref, live_ref, oq_ref, dkv_ref):
    queries = BAND_ROWS * TILE
    keys = KEY_ROWS * WINDOW
    c0 = pl.multiple_of(i * TILE, TILE)
    at = pl.multiple_of(i * TILE + TILE // 2, TILE // 2)
    kv = kv_ref[:, pl.ds(c0, WINDOW), :].reshape(keys, 128)
    feat = feat_ref[:, pl.ds(c0, WINDOW), :].reshape(keys, 128)
    q = q_ref[:, pl.ds(at, TILE), :].reshape(queries, 128).astype(jnp.bfloat16)
    g = g_ref[:, pl.ds(at, TILE), :].reshape(queries, 128).astype(jnp.bfloat16)
    pick = pick_ref[lax.rem(i, 2)]
    both = jnp.concatenate(
        [
            jnp.concatenate([q, pick], axis=1),
            jnp.concatenate([g, jnp.zeros_like(g)], axis=1),
        ],
        axis=0,
    )
    products = lax.dot_general(
        jnp.concatenate([kv, feat], axis=1),
        both,
        (((1,), (1,)), ((), ())),
        preferred_element_type=jnp.float32,
    )
    scores = products[:, :queries]
    grad_probs = products[:, queries:]
    highest = jnp.max(scores, axis=0, keepdims=True)
    terms = jnp.exp(scores - highest)
    probs = terms * (live_ref[i] / jnp.sum(terms, axis=0, keepdims=True))
    weights = probs.astype(jnp.bfloat16)
    row_delta = jnp.sum(probs * grad_probs, axis=0, keepdims=True)
    grad_scores = (probs * (grad_probs - row_delta)).astype(jnp.bfloat16)
    pair = jnp.concatenate([weights, grad_scores], axis=1)
    dkv = jnp.dot(pair, jnp.concatenate([g, q], axis=0), preferred_element_type=jnp.float32)
    dkv_ref[:, pl.ds(c0, WINDOW), :] += dkv.reshape(KEY_ROWS, WINDOW, 128)
    out = lax.dot_general(
        pair, kv, (((0,), (0,)), ((), ())), preferred_element_type=jnp.float32
    )
    lane = lax.broadcasted_iota(jnp.int32, (queries, 128), 1)
    oq = jnp.where(lane < HEAD_WIDTH, out[queries:] * (1.0 / math.sqrt(HEAD_WIDTH)), out[:queries])
    oq_ref[:, pl.ds(at, TILE), :] = oq.reshape(BAND_ROWS, TILE, 128)


def attention_kernel(kv_ref, feat_ref, q_ref, g_ref, pick_ref, live_ref, oq_ref, dkv_ref):
    dkv_ref[...] = jnp.zeros_like(dkv_ref)

    @pl.loop(0, TILES)
    def _(i):
        attention_tile(i, kv_ref, feat_ref, q_ref, g_ref, pick_ref, live_ref, oq_ref, dkv_ref)

    half = TILE // 2
    oq_ref[:, :half, :] = oq_ref[:, LONGITUDES : LONGITUDES + half, :]
    dkv_ref[:, :TILE, :] += dkv_ref[:, LONGITUDES : LONGITUDES + TILE, :]


def attention(kv, feat, q, g, pick, live):
    return pl.pallas_call(
        attention_kernel,
        out_shape=(
            jax.ShapeDtypeStruct((BAND_ROWS, QUERY_COLS, 128), jnp.float32),
            jax.ShapeDtypeStruct((KEY_ROWS, KEY_COLS, 128), jnp.float32),
        ),
        in_specs=[pl.BlockSpec(memory_space=VMEM)] * 6,
        out_specs=[pl.BlockSpec(memory_space=VMEM)] * 2,
        compiler_params=pltpu.CompilerParams(vmem_limit_bytes=48 << 20),
        name="attention",
    )(kv, feat, q, g, pick, live)


def on_device(tokens, gain, qkv_weight, out_weight, row_cells, upstream):
    band_tokens = BAND_ROWS * LONGITUDES
    score_scale = 1.0 / math.sqrt(HEAD_WIDTH)
    grad_scale = 4.0 / math.sqrt(band_tokens * lax.axis_size("lat"))
    band_start = lax.axis_index("lat") * BAND_ROWS
    features = tokens.astype(jnp.float32)
    inverse = lax.rsqrt(jnp.mean(features * features, axis=1, keepdims=True) + 1e-06)
    normed = (features * inverse * gain[None, :]).astype(jnp.bfloat16)
    normed_band = lax.all_gather(normed, "mp", axis=0, tiled=True)
    cells = lax.dynamic_slice_in_dim(jnp.pad(row_cells, (REACH, REACH)), band_start, KEY_ROWS)
    qkv_flat = qkv_weight.reshape(3 * HEAD_WIDTH, WIDTH)
    qkv = lax.dot_general(
        normed_band, qkv_flat, (((1,), (1,)), ((), ())), preferred_element_type=jnp.float32
    ).astype(jnp.bfloat16)
    qkv = qkv.reshape(BAND_ROWS, LONGITUDES, 3 * HEAD_WIDTH)
    kv = qkv[..., HEAD_WIDTH:]
    before = passed_along(kv[BAND_ROWS - REACH :], "lat", 1)
    after = passed_along(kv[:REACH], "lat", -1)
    kv_all = jnp.concatenate([before, kv, after], axis=0)
    kv_all = jnp.concatenate([kv_all, kv_all[:, :TILE]], axis=1)
    out_flat = out_weight.reshape(HEAD_WIDTH, WIDTH)
    band_upstream = lax.all_gather(upstream, "mp", axis=0, tiled=True)
    grad_heads = lax.dot_general(
        band_upstream, out_flat, (((1,), (1,)), ((), ())), preferred_element_type=jnp.float32
    ).astype(jnp.bfloat16)
    half = TILE // 2
    q = jnp.pad(qkv[..., :HEAD_WIDTH].astype(jnp.float32) * score_scale, ((0, 0), (0, 0), (0, HEAD_WIDTH)))
    q = jnp.concatenate([q, q[:, :half]], axis=1)
    g = grad_heads.astype(jnp.float32).reshape(BAND_ROWS, LONGITUDES, HEAD_WIDTH)
    g = jnp.pad(g, ((0, 0), (0, 0), (HEAD_WIDTH, 0)))
    g = jnp.concatenate([g, g[:, :half]], axis=1)
    oq, dkv = attention(kv_all, key_features(cells), q, g, query_features(), live_queries(cells))
    oq = oq[:, :LONGITUDES].astype(jnp.bfloat16).reshape(band_tokens, 128)
    heads_out = oq[:, HEAD_WIDTH:]
    update = lax.psum_scatter(
        jnp.dot(heads_out, out_flat, preferred_element_type=jnp.float32).astype(jnp.bfloat16),
        "mp",
        scatter_dimension=0,
        tiled=True,
    )
    grad_out_part = lax.dot_general(
        heads_out, band_upstream, (((0,), (0,)), ((), ())), preferred_element_type=jnp.float32
    )
    dkv = dkv[:, :LONGITUDES]
    from_above = passed_along(dkv[:REACH], "lat", -1)
    from_below = passed_along(dkv[BAND_ROWS + REACH :], "lat", 1)
    own = dkv[REACH : BAND_ROWS + REACH]
    own = own.at[:REACH].add(from_below).at[BAND_ROWS - REACH :].add(from_above)
    grad_kv = own.astype(jnp.bfloat16).reshape(band_tokens, 2 * HEAD_WIDTH)
    grad_proj = jnp.concatenate([oq[:, :HEAD_WIDTH], grad_kv], axis=1)
    grad_qkv_part = lax.dot_general(
        grad_proj, normed_band, (((0,), (0,)), ((), ())), preferred_element_type=jnp.float32
    )
    grad_qkv, grad_out = lax.psum((grad_qkv_part, grad_out_part), "lat")
    grad_normed = lax.psum_scatter(
        jnp.dot(grad_proj, qkv_flat, preferred_element_type=jnp.float32).astype(jnp.bfloat16),
        "mp",
        scatter_dimension=0,
        tiled=True,
    ).astype(jnp.float32)
    centred = features * inverse
    scaled = gain[None, :] * grad_normed
    grad_input = inverse * (scaled - centred * jnp.mean(scaled * centred, axis=1, keepdims=True))
    return (
        update.astype(jnp.bfloat16),
        grad_input.astype(jnp.bfloat16),
        (grad_qkv * grad_scale).reshape(1, 3 * HEAD_WIDTH, WIDTH),
        (grad_out * grad_scale).reshape(1, HEAD_WIDTH, WIDTH),
    )


def solution(mesh):
    return jax.shard_map(
        on_device,
        mesh=mesh,
        in_specs=(
            P(("lat", "mp"), None),
            P(),
            P("mp", None, None),
            P("mp", None, None),
            P(),
            P(("lat", "mp"), None),
        ),
        out_specs=(
            P(("lat", "mp"), None),
            P(("lat", "mp"), None),
            P("mp", None, None),
            P("mp", None, None),
        ),
        check_vma=False,
    )
```

```python
import math

import jax
import jax.numpy as jnp
from jax import lax
from jax.experimental import pallas as pl
from jax.experimental.pallas import tpu as pltpu
from jax.sharding import PartitionSpec as P

WIDTH = 1024
HEAD_WIDTH = 64
LONGITUDES = 256
BAND_ROWS = 8
REACH = 6
KEY_ROWS = BAND_ROWS + 2 * REACH
TILE = 16
WINDOW = 2 * TILE
TILES = LONGITUDES // TILE
KEY_COLS = LONGITUDES + TILE
QUERY_COLS = LONGITUDES + TILE // 2
NEVER = -1e30
VMEM = pltpu.VMEM
MESH = pl.DeviceIdType.MESH
HALF = LONGITUDES // 2
BF = jnp.bfloat16
F32 = jnp.float32
DMA = pltpu.SemaphoreType.DMA


def key_features(cells):
    shape = (KEY_ROWS, KEY_COLS, 128)
    row = lax.broadcasted_iota(jnp.int32, shape, 0)
    col = lax.broadcasted_iota(jnp.int32, shape, 1)
    lane = lax.broadcasted_iota(jnp.int32, shape, 2)
    live = col % LONGITUDES < cells[:, None, None]
    near_row = (row >= lane - 8) & (row <= lane - 8 + 2 * REACH)
    apart = (col - lane) % 32
    near_col = (apart <= REACH) | (apart >= 32 - REACH)
    barred = (
        ((lane == 0) & ~live)
        | ((lane >= 8) & (lane < 16) & ~near_row)
        | ((lane >= 32) & (lane < 64) & ~near_col)
    )
    return jnp.where(barred, NEVER, 0.0).astype(jnp.bfloat16)


def query_features():
    shape = (2, BAND_ROWS, TILE, 128)
    tile, row, col, lane = (lax.broadcasted_iota(jnp.int32, shape, d) for d in range(4))
    picked = (
        (lane == 0)
        | (lane == 8 + row)
        | (lane == 32 + (TILE * tile + TILE // 2 + col) % 32)
    )
    return picked.astype(jnp.bfloat16).reshape(2, BAND_ROWS * TILE, 128)


def live_queries(cells):
    shape = (TILES, 1, BAND_ROWS, TILE)
    tile, _, _, col = (lax.broadcasted_iota(jnp.int32, shape, d) for d in range(4))
    at = (TILE * tile + TILE // 2 + col) % LONGITUDES
    live = at < cells[REACH : REACH + BAND_ROWS][None, None, :, None]
    return live.astype(jnp.float32).reshape(TILES, 1, BAND_ROWS * TILE)


def attention_tile(i, kv_ref, feat_ref, q_ref, g_ref, pick_ref, live_ref, oq_ref, dkv_ref):
    queries = BAND_ROWS * TILE
    keys = KEY_ROWS * WINDOW
    c0 = pl.multiple_of(i * TILE, TILE)
    at = pl.multiple_of(i * TILE + TILE // 2, TILE // 2)
    kv = kv_ref[:, pl.ds(c0, WINDOW), :].reshape(keys, 128)
    feat = feat_ref[:, pl.ds(c0, WINDOW), :].reshape(keys, 128)
    q = q_ref[:, pl.ds(at, TILE), :].reshape(queries, 128).astype(jnp.bfloat16)
    g = g_ref[:, pl.ds(at, TILE), :].reshape(queries, 128).astype(jnp.bfloat16)
    pick = pick_ref[lax.rem(i, 2)]
    both = jnp.concatenate(
        [
            jnp.concatenate([q, pick], axis=1),
            jnp.concatenate([g, jnp.zeros_like(g)], axis=1),
        ],
        axis=0,
    )
    products = lax.dot_general(
        jnp.concatenate([kv, feat], axis=1),
        both,
        (((1,), (1,)), ((), ())),
        preferred_element_type=jnp.float32,
    )
    scores = products[:, :queries]
    grad_probs = products[:, queries:]
    highest = jnp.max(scores, axis=0, keepdims=True)
    terms = jnp.exp(scores - highest)
    probs = terms * (live_ref[i] / jnp.sum(terms, axis=0, keepdims=True))
    weights = probs.astype(jnp.bfloat16)
    row_delta = jnp.sum(probs * grad_probs, axis=0, keepdims=True)
    grad_scores = (probs * (grad_probs - row_delta)).astype(jnp.bfloat16)
    pair = jnp.concatenate([weights, grad_scores], axis=1)
    dkv = jnp.dot(pair, jnp.concatenate([g, q], axis=0), preferred_element_type=jnp.float32)
    dkv_ref[:, pl.ds(c0, WINDOW), :] += dkv.reshape(KEY_ROWS, WINDOW, 128)
    out = lax.dot_general(
        pair, kv, (((0,), (0,)), ((), ())), preferred_element_type=jnp.float32
    )
    lane = lax.broadcasted_iota(jnp.int32, (queries, 128), 1)
    oq = jnp.where(lane < HEAD_WIDTH, out[queries:] * (1.0 / math.sqrt(HEAD_WIDTH)), out[:queries])
    oq_ref[:, pl.ds(at, TILE), :] = oq.reshape(BAND_ROWS, TILE, 128)


def remote(src, dst, send_sem, recv_sem, device):
    return pltpu.make_async_remote_copy(
        src_ref=src,
        dst_ref=dst,
        send_sem=send_sem,
        recv_sem=recv_sem,
        device_id=device,
        device_id_type=MESH,
    )


def sublayer_kernel(
    tok_ref, gain_ref, w_ref, wo_ref, up_ref, feat_ref, pick_ref, live_ref,
    update_ref, grad_in_ref, grad_qkv_ref, grad_out_ref,
    nb, ub, wp, wo, kv, q, g, oq, dkv, hs, hr, ab, asib, us, ur, gs, gr, mine, wg, wgb, lr, lf,
    sn, rn, snf, rnf, su, ru, suf, ruf, sw, rw, sh, rh, shg, rhg, sa, ra, sup, rup, sgn, rgn, sl, rl, sf, rf,
):
    lat, mp = lax.axis_index("lat"), lax.axis_index("mp")
    y, x, core = mp // 8, (mp // 2) % 4, mp % 2
    me = mp // 2
    sibling = {"mp": me * 2 + (1 - core)}
    own_half = pl.ds(pl.multiple_of(core * HALF, HALF), HALF)
    other_half = pl.ds(pl.multiple_of((1 - core) * HALF, HALF), HALF)

    def chip(k):
        d = k % 4
        d = d + (d // 2) * (1 - 2 * (d % 2))
        return ((y + k // 4) % 2) * 4 + (x + d) % 4

    def peer(row):
        return {"mp": row * 2 + core}

    def along(step):
        return {"lat": (lat + step) % 16}

    barrier = pltpu.get_barrier_semaphore()

    @pl.loop(1, 8)
    def _(k):
        pl.semaphore_signal(barrier, inc=1, device_id=peer(chip(k)), device_id_type=MESH)

    pl.semaphore_signal(barrier, inc=1, device_id=sibling, device_id_type=MESH)

    @pl.loop(1, 16)
    def _(k):
        pl.semaphore_signal(barrier, inc=1, device_id=along(k), device_id_type=MESH)

    def normalised():
        features = tok_ref[...].astype(F32)
        inverse = lax.rsqrt(jnp.mean(features * features, axis=1, keepdims=True) + 1e-06)
        return features, inverse

    features, inverse = normalised()
    nb[me, own_half, :] = (features * inverse * gain_ref[...]).astype(BF)
    ub[me, own_half, :] = up_ref[...]
    wp[0:64, :] = w_ref[0:64, :]
    wp[64:128, :] = jnp.zeros((64, WIDTH), BF)
    wp[128:256, :] = w_ref[64:192, :]
    wo[0:64, :] = jnp.zeros((64, WIDTH), BF)
    wo[64:128, :] = wo_ref[...]
    pl.semaphore_wait(barrier, 23)

    def spread(buf, s, r, k):
        return remote(buf.at[me, own_half], buf.at[me, own_half], s.at[k], r.at[me], peer(chip(k)))

    def arrived(buf, s, r, row):
        return remote(buf.at[row, own_half], buf.at[row, own_half], s.at[0], r.at[row], peer(row))

    def handed(buf, s, r, row):
        return remote(buf.at[row, own_half], buf.at[row, own_half], s.at[row], r.at[row], sibling)

    def handed_in(buf, s, r, row):
        return remote(buf.at[row, other_half], buf.at[row, other_half], s.at[row], r.at[row], sibling)

    @pl.loop(1, 8)
    def _(k):
        spread(nb, sn, rn, k).start()

    handed(nb, snf, rnf, me).start()
    handed(ub, suf, ruf, me).start()
    weights_over = remote(wp.at[0:256], wp.at[256:512], sw.at[0], rw.at[0], sibling)
    weights_over.start()
    out_weights_over = remote(wo.at[0:128], wo.at[128:256], sw.at[1], rw.at[1], sibling)
    out_weights_over.start()
    dkv[...] = jnp.zeros_like(dkv)

    def project(row):
        handed_in(nb, snf, rnf, row).wait_recv()
        made = lax.dot_general(
            nb[row], wp[0:256, :], (((1,), (1,)), ((), ())), preferred_element_type=F32
        ).astype(BF)
        scaled = made[:, 0:128].astype(F32) * (1.0 / math.sqrt(HEAD_WIDTH))
        q[row, 0:LONGITUDES, :] = scaled
        q[row, LONGITUDES:QUERY_COLS, :] = scaled[0 : TILE // 2]
        kv[REACH + row, 0:LONGITUDES, :] = made[:, 128:256]
        kv[REACH + row, LONGITUDES:KEY_COLS, :] = made[0:TILE, 128:256]

    def project_upstream(row):
        handed_in(ub, suf, ruf, row).wait_recv()
        made = lax.dot_general(
            ub[row], wo[0:128, :], (((1,), (1,)), ((), ())), preferred_element_type=F32
        ).astype(BF)
        made = made.astype(F32)
        g[row, 0:LONGITUDES, :] = made
        g[row, LONGITUDES:QUERY_COLS, :] = made[0 : TILE // 2]

    @pl.loop(1, 8)
    def _(k):
        row = chip(k)
        arrived(nb, sn, rn, row).wait_recv()
        handed(nb, snf, rnf, row).start()
        project(chip(k - 1))
        spread(nb, sn, rn, k).wait_send()
        spread(ub, su, ru, k).start()

    project(chip(7))

    up_halo = remote(kv.at[BAND_ROWS : BAND_ROWS + REACH], kv.at[0:REACH], sh.at[0], rh.at[0], along(1))
    up_halo.start()
    down_halo = remote(kv.at[REACH : 2 * REACH], kv.at[BAND_ROWS + REACH : KEY_ROWS], sh.at[1], rh.at[1], along(15))
    down_halo.start()

    @pl.loop(1, 8)
    def _(k):
        row = chip(k)
        arrived(ub, su, ru, row).wait_recv()
        handed(ub, suf, ruf, row).start()
        project_upstream(chip(k - 1))

    project_upstream(chip(7))
    up_halo.wait()
    down_halo.wait()

    @pl.loop(0, TILES)
    def _(i):
        attention_tile(i, kv, feat_ref, q, g, pick_ref, live_ref, oq, dkv)

    half = TILE // 2
    oq[:, :half, :] = oq[:, LONGITUDES : LONGITUDES + half, :]
    dkv[:, :TILE, :] += dkv[:, LONGITUDES : LONGITUDES + TILE, :]
    hs[0] = dkv[0:REACH, 0:LONGITUDES, :].astype(BF)
    hs[1] = dkv[BAND_ROWS + REACH : KEY_ROWS, 0:LONGITUDES, :].astype(BF)
    down_grad = remote(hs.at[0], hr.at[0], shg.at[0], rhg.at[0], along(15))
    down_grad.start()
    up_grad = remote(hs.at[1], hr.at[1], shg.at[1], rhg.at[1], along(1))
    up_grad.start()
    ab[:, :, 0:128] = oq[:, 0:LONGITUDES, :].astype(BF)
    oq_over = remote(ab.at[:, other_half, 0:128], asib.at[:, :, 0:128], sa.at[0], ra.at[0], sibling)
    oq_over.start()

    columns = 512

    @pl.loop(0, WIDTH // columns)
    def _(n):
        cut = pl.ds(pl.multiple_of(n * columns, columns), columns)
        part = lax.dot_general(
            ab[:, :, 0:128].reshape(BAND_ROWS * LONGITUDES, 128),
            ub[:, :, cut].reshape(BAND_ROWS * LONGITUDES, columns),
            (((0,), (0,)), ((), ())),
            preferred_element_type=F32,
        )
        wg[192:256, cut] = part[64:128]

    out_weights_over.wait()
    oq_over.wait()

    def sent(buf, into, s, r, k):
        row = chip(k)
        return remote(buf.at[row], into.at[me], s.at[k], r.at[me], peer(row))

    def received(into, s, r, row):
        return remote(into.at[row], into.at[row], s.at[0], r.at[row], peer(row))

    def update_part(row):
        both = jnp.concatenate([ab[row, own_half, 0:128], asib[row, :, 0:128]], axis=1)
        return jnp.dot(both, wo[...], preferred_element_type=F32)

    @pl.loop(1, 8)
    def _(k):
        us[chip(k)] = update_part(chip(k)).astype(BF)
        sent(us, ur, sup, rup, k).start()

    mine[0] = update_part(me)
    down_grad.wait()
    up_grad.wait()
    dkv[BAND_ROWS : BAND_ROWS + REACH, 0:LONGITUDES, :] += hr[0].astype(F32)
    dkv[REACH : 2 * REACH, 0:LONGITUDES, :] += hr[1].astype(F32)
    ab[:, :, 128:256] = dkv[REACH : REACH + BAND_ROWS, 0:LONGITUDES, :].astype(BF)
    kv_over = remote(ab.at[:, other_half, 128:256], asib.at[:, :, 128:256], sa.at[1], ra.at[1], sibling)
    kv_over.start()
    weights_over.wait()
    kv_over.wait()

    def grad_part(row):
        both = jnp.concatenate([ab[row, own_half, :], asib[row]], axis=1)
        return jnp.dot(both, wp[...], preferred_element_type=F32)

    @pl.loop(1, 8)
    def _(k):
        gs[chip(k)] = grad_part(chip(k)).astype(BF)
        sent(gs, gr, sgn, rgn, k).start()

    mine[1] = grad_part(me)

    @pl.loop(0, WIDTH // columns)
    def _(n):
        cut = pl.ds(pl.multiple_of(n * columns, columns), columns)
        part = lax.dot_general(
            ab[...].reshape(BAND_ROWS * LONGITUDES, 256),
            nb[:, :, cut].reshape(BAND_ROWS * LONGITUDES, columns),
            (((0,), (0,)), ((), ())),
            preferred_element_type=F32,
        )
        wg[0:64, cut] = part[0:64]
        wg[64:192, cut] = part[128:256]

    wgb[...] = wg[...].astype(BF)

    def share(row):
        return pl.ds(pl.multiple_of(row * 16, 16), 16)

    def scatter(k):
        to = (lat + k) % 16
        return remote(wgb.at[share(to)], lr.at[k], sl.at[k], rl.at[k], along(k))

    def gather(k):
        return remote(lf.at[share(lat)], lf.at[share(lat)], sf.at[k], rf.at[k], along(k))

    def gathered(k):
        row = (lat + 16 - k) % 16
        return remote(lf.at[share(row)], lf.at[share(row)], sf.at[k], rf.at[k], along(k))

    @pl.loop(1, 16)
    def _(k):
        scatter(k).start()

    lr[0] = wgb[share(lat), :]
    total = wg[share(lat), :]
    for k in range(1, 16):
        scatter(k).wait()
        total = total + lr[k].astype(F32)
    lf[share(lat), :] = (total * (4.0 / math.sqrt(BAND_ROWS * LONGITUDES * 16))).astype(BF)

    @pl.loop(1, 16)
    def _(k):
        gather(k).start()

    total = mine[0]
    for k in range(1, 8):
        received(ur, sup, rup, chip(k)).wait_recv()
        total = total + ur[chip(k)].astype(F32)
    update_ref[...] = total.astype(BF)

    total = mine[1]
    for k in range(1, 8):
        received(gr, sgn, rgn, chip(k)).wait_recv()
        total = total + gr[chip(k)].astype(F32)
    features, inverse = normalised()
    centred = features * inverse
    scaled = gain_ref[...] * total
    grad_in_ref[...] = (
        inverse * (scaled - centred * jnp.mean(scaled * centred, axis=1, keepdims=True))
    ).astype(BF)

    @pl.loop(1, 16)
    def _(k):
        gather(k).wait_send()
        gathered(k).wait_recv()

    grad_qkv_ref[...] = lf[0:192, :].astype(F32)
    grad_out_ref[...] = lf[192:256, :].astype(F32)

    @pl.loop(1, 8)
    def _(k):
        spread(ub, su, ru, k).wait_send()
        sent(us, ur, sup, rup, k).wait_send()
        sent(gs, gr, sgn, rgn, k).wait_send()

    @pl.loop(0, 8)
    def _(k):
        handed(nb, snf, rnf, k).wait_send()
        handed(ub, suf, ruf, k).wait_send()


def on_device(tokens, gain, qkv_weight, out_weight, row_cells, upstream):
    band_start = lax.axis_index("lat") * BAND_ROWS
    cells = lax.dynamic_slice_in_dim(jnp.pad(row_cells, (REACH, REACH)), band_start, KEY_ROWS)
    shape = (BAND_ROWS, LONGITUDES, WIDTH)
    queries = (BAND_ROWS, QUERY_COLS, 128)
    keys = (KEY_ROWS, KEY_COLS, 128)
    halo = (2, REACH, LONGITUDES, 128)
    blocks = (8, HALF, WIDTH)
    update, grad_input, grad_qkv, grad_out = pl.pallas_call(
        sublayer_kernel,
        out_shape=(
            jax.ShapeDtypeStruct((HALF, WIDTH), BF),
            jax.ShapeDtypeStruct((HALF, WIDTH), BF),
            jax.ShapeDtypeStruct((3 * HEAD_WIDTH, WIDTH), F32),
            jax.ShapeDtypeStruct((HEAD_WIDTH, WIDTH), F32),
        ),
        in_specs=[pl.BlockSpec(memory_space=VMEM)] * 8,
        out_specs=[pl.BlockSpec(memory_space=VMEM)] * 4,
        scratch_shapes=[
            VMEM(shape, BF),
            VMEM(shape, BF),
            VMEM((512, WIDTH), BF),
            VMEM((256, WIDTH), BF),
            VMEM(keys, BF),
            VMEM(queries, F32),
            VMEM(queries, F32),
            VMEM(queries, F32),
            VMEM(keys, F32),
            VMEM(halo, BF),
            VMEM(halo, BF),
            VMEM((BAND_ROWS, LONGITUDES, 256), BF),
            VMEM((BAND_ROWS, HALF, 256), BF),
            VMEM(blocks, BF),
            VMEM(blocks, BF),
            VMEM(blocks, BF),
            VMEM(blocks, BF),
            VMEM((2, HALF, WIDTH), F32),
            VMEM((256, WIDTH), F32),
            VMEM((256, WIDTH), BF),
            VMEM((16, 16, WIDTH), BF),
            VMEM((256, WIDTH), BF),
        ]
        + [DMA((8,))] * 8
        + [DMA((2,))] * 8
        + [DMA((8,))] * 4
        + [DMA((16,))] * 4,
        compiler_params=pltpu.CompilerParams(
            collective_id=0, has_side_effects=True, vmem_limit_bytes=56 << 20
        ),
        name="sublayer",
    )(
        tokens,
        gain.reshape(1, WIDTH),
        qkv_weight.reshape(3 * HEAD_WIDTH, WIDTH),
        out_weight.reshape(HEAD_WIDTH, WIDTH),
        upstream,
        key_features(cells),
        query_features(),
        live_queries(cells),
    )
    return (
        update,
        grad_input,
        grad_qkv.reshape(1, 3 * HEAD_WIDTH, WIDTH),
        grad_out.reshape(1, HEAD_WIDTH, WIDTH),
    )


def solution(mesh):
    return jax.shard_map(
        on_device,
        mesh=mesh,
        in_specs=(
            P(("lat", "mp"), None),
            P(),
            P("mp", None, None),
            P("mp", None, None),
            P(),
            P(("lat", "mp"), None),
        ),
        out_specs=(
            P(("lat", "mp"), None),
            P(("lat", "mp"), None),
            P("mp", None, None),
            P("mp", None, None),
        ),
        check_vma=False,
    )
```

```python
import math

import jax
import jax.numpy as jnp
from jax import lax
from jax.experimental import pallas as pl
from jax.experimental.pallas import tpu as pltpu
from jax.sharding import PartitionSpec as P

WIDTH = 1024
HEAD_WIDTH = 64
LONGITUDES = 256
BAND_ROWS = 8
REACH = 6
KEY_ROWS = BAND_ROWS + 2 * REACH
TILE = 16
WINDOW = 2 * TILE
TILES = LONGITUDES // TILE
KEY_COLS = LONGITUDES + TILE
QUERY_COLS = LONGITUDES + TILE // 2
NEVER = -1e30
VMEM = pltpu.VMEM
MESH = pl.DeviceIdType.MESH
HALF = LONGITUDES // 2
BF = jnp.bfloat16
F32 = jnp.float32
DMA = pltpu.SemaphoreType.DMA


def key_features(cells):
    shape = (KEY_ROWS, KEY_COLS, 128)
    row = lax.broadcasted_iota(jnp.int32, shape, 0)
    col = lax.broadcasted_iota(jnp.int32, shape, 1)
    lane = lax.broadcasted_iota(jnp.int32, shape, 2)
    live = col % LONGITUDES < cells[:, None, None]
    near_row = (row >= lane - 8) & (row <= lane - 8 + 2 * REACH)
    apart = (col - lane) % 32
    near_col = (apart <= REACH) | (apart >= 32 - REACH)
    barred = (
        ((lane == 0) & ~live)
        | ((lane >= 8) & (lane < 16) & ~near_row)
        | ((lane >= 32) & (lane < 64) & ~near_col)
    )
    return jnp.where(barred, NEVER, 0.0).astype(jnp.bfloat16)


def query_features():
    shape = (2, BAND_ROWS, TILE, 128)
    tile, row, col, lane = (lax.broadcasted_iota(jnp.int32, shape, d) for d in range(4))
    picked = (
        (lane == 0)
        | (lane == 8 + row)
        | (lane == 32 + (TILE * tile + TILE // 2 + col) % 32)
    )
    return picked.astype(jnp.bfloat16).reshape(2, BAND_ROWS * TILE, 128)


def live_queries(cells):
    shape = (TILES, 1, BAND_ROWS, TILE)
    tile, _, _, col = (lax.broadcasted_iota(jnp.int32, shape, d) for d in range(4))
    at = (TILE * tile + TILE // 2 + col) % LONGITUDES
    live = at < cells[REACH : REACH + BAND_ROWS][None, None, :, None]
    return live.astype(jnp.float32).reshape(TILES, 1, BAND_ROWS * TILE)


def attention_tile(i, kv_ref, feat_ref, q_ref, g_ref, pick_ref, live_ref, oq_ref, dkv_ref):
    queries = BAND_ROWS * TILE
    keys = KEY_ROWS * WINDOW
    c0 = pl.multiple_of(i * TILE, TILE)
    at = pl.multiple_of(i * TILE + TILE // 2, TILE // 2)
    kv = kv_ref[:, pl.ds(c0, WINDOW), :].reshape(keys, 128)
    feat = feat_ref[:, pl.ds(c0, WINDOW), :].reshape(keys, 128)
    q = q_ref[:, pl.ds(at, TILE), :].reshape(queries, 128).astype(jnp.bfloat16)
    g = g_ref[:, pl.ds(at, TILE), :].reshape(queries, 128).astype(jnp.bfloat16)
    pick = pick_ref[lax.rem(i, 2)]
    both = jnp.concatenate(
        [
            jnp.concatenate([q, pick], axis=1),
            jnp.concatenate([g, jnp.zeros_like(g)], axis=1),
        ],
        axis=0,
    )
    products = lax.dot_general(
        jnp.concatenate([kv, feat], axis=1),
        both,
        (((1,), (1,)), ((), ())),
        preferred_element_type=jnp.float32,
    )
    scores = products[:, :queries]
    grad_probs = products[:, queries:]
    highest = jnp.max(scores, axis=0, keepdims=True)
    terms = jnp.exp(scores - highest)
    probs = terms * (live_ref[i] / jnp.sum(terms, axis=0, keepdims=True))
    weights = probs.astype(jnp.bfloat16)
    row_delta = jnp.sum(probs * grad_probs, axis=0, keepdims=True)
    grad_scores = (probs * (grad_probs - row_delta)).astype(jnp.bfloat16)
    pair = jnp.concatenate([weights, grad_scores], axis=1)
    dkv = jnp.dot(pair, jnp.concatenate([g, q], axis=0), preferred_element_type=jnp.float32)
    dkv_ref[:, pl.ds(c0, WINDOW), :] += dkv.reshape(KEY_ROWS, WINDOW, 128)
    out = lax.dot_general(
        pair, kv, (((0,), (0,)), ((), ())), preferred_element_type=jnp.float32
    )
    lane = lax.broadcasted_iota(jnp.int32, (queries, 128), 1)
    oq = jnp.where(lane < HEAD_WIDTH, out[queries:] * (1.0 / math.sqrt(HEAD_WIDTH)), out[:queries])
    oq_ref[:, pl.ds(at, TILE), :] = oq.reshape(BAND_ROWS, TILE, 128)


def remote(src, dst, send_sem, recv_sem, device):
    return pltpu.make_async_remote_copy(
        src_ref=src,
        dst_ref=dst,
        send_sem=send_sem,
        recv_sem=recv_sem,
        device_id=device,
        device_id_type=MESH,
    )


def sublayer_kernel(
    tok_ref, gain_ref, w_ref, wo_ref, up_ref, feat_ref, pick_ref, live_ref,
    update_ref, grad_in_ref, grad_qkv_ref, grad_out_ref,
    nb, ub, wp, wall, kv, q, g, oq, dkv, hs, hr, ab, asib, ds, gb, os, oa, gs, gr, gy, mine, wg, wgb, wx, lr, lf,
    sn, rn, snf, rnf, su, ru, sw, rw, swf, rwf, sku, rku, skd, rkd, shg, rhg, so, ro, sgn, rgn,
    sd, rd, sl, rl, sf, rf, sp, rp,
):
    lat, mp = lax.axis_index("lat"), lax.axis_index("mp")
    y, x, core = mp // 8, (mp // 2) % 4, mp % 2
    me = mp // 2
    across = (1 - y) * 4 + x
    sibling = {"mp": me * 2 + (1 - core)}

    def halves(width):
        return (
            pl.ds(pl.multiple_of(core * width, width), width),
            pl.ds(pl.multiple_of((1 - core) * width, width), width),
        )

    own_half, other_half = halves(HALF)
    own_head, other_head = halves(HEAD_WIDTH)

    def chip(k):
        d = k % 4
        d = d + (d // 2) * (1 - 2 * (d % 2))
        return ((y + k // 4) % 2) * 4 + (x + d) % 4

    def peer(row):
        return {"mp": row * 2 + core}

    def along(step):
        return {"lat": (lat + step) % 16}

    barrier = pltpu.get_barrier_semaphore()

    @pl.loop(1, 16)
    def _(k):
        pl.semaphore_signal(barrier, inc=1, device_id={"mp": (mp + k) % 16}, device_id_type=MESH)
        pl.semaphore_signal(barrier, inc=1, device_id=along(k), device_id_type=MESH)

    def normalised():
        features = tok_ref[...].astype(F32)
        inverse = lax.rsqrt(jnp.mean(features * features, axis=1, keepdims=True) + 1e-06)
        return features, inverse

    features, inverse = normalised()
    nb[me, own_half, :] = (features * inverse * gain_ref[...]).astype(BF)
    ub[me] = up_ref[...]
    wall[me, own_head, :] = wo_ref[...]
    wp[0:64, :] = w_ref[0:64, :]
    wp[64:128, :] = jnp.zeros((64, WIDTH), BF)
    wp[128:256, :] = w_ref[64:192, :]
    pl.semaphore_wait(barrier, 30)

    def blocks(buf, cut, s, r):
        def at(row):
            return buf.at[row] if cut is None else buf.at[row, cut]

        def own(k):
            return remote(at(me), at(me), s.at[k], r.at[me], peer(chip(k)))

        def passed(k):
            return remote(at(across), at(across), s.at[k + 4], r.at[across], peer(chip(k)))

        def arrived(row):
            return remote(at(row), at(row), s.at[0], r.at[row], peer(row))

        return own, passed, arrived

    def handing(buf, cut, cut_in, s, r):
        def out(row):
            return remote(buf.at[row, cut], buf.at[row, cut], s.at[row], r.at[row], sibling)

        def into(row):
            return remote(buf.at[row, cut_in], buf.at[row, cut_in], s.at[row], r.at[row], sibling)

        return out, into

    n_own, n_passed, n_arrived = blocks(nb, own_half, sn, rn)
    n_out, n_in = handing(nb, own_half, other_half, snf, rnf)
    w_own, w_passed, w_arrived = blocks(wall, own_head, sw, rw)
    w_out, w_in = handing(wall, own_head, other_head, swf, rwf)
    u_own, u_passed, u_arrived = blocks(ub, None, su, ru)

    n_own(4).start()

    @pl.loop(1, 4)
    def _(k):
        n_own(k).start()

    n_out(me).start()
    w_out(me).start()
    weights_over = remote(wp.at[0:256], wp.at[256:512], sp.at[0], rp.at[0], sibling)
    weights_over.start()
    dkv[...] = jnp.zeros_like(dkv)

    def up_halo(row):
        return remote(kv.at[REACH + row], kv.at[row + REACH - BAND_ROWS], sku.at[row], rku.at[row], along(1))

    def down_halo(row):
        return remote(kv.at[REACH + row], kv.at[row + REACH + BAND_ROWS], skd.at[row], rkd.at[row], along(15))

    def project(row):
        n_in(row).wait_recv()
        made = lax.dot_general(
            nb[row], wp[0:256, :], (((1,), (1,)), ((), ())), preferred_element_type=F32
        ).astype(BF)
        kv[REACH + row, 0:LONGITUDES, :] = made[:, 128:256]
        kv[REACH + row, LONGITUDES:KEY_COLS, :] = made[0:TILE, 128:256]

        @pl.when(row >= BAND_ROWS - REACH)
        def _():
            up_halo(row).start()

        @pl.when(row < REACH)
        def _():
            down_halo(row).start()

        scaled = made[:, 0:128].astype(F32) * (1.0 / math.sqrt(HEAD_WIDTH))
        q[row, 0:LONGITUDES, :] = scaled
        q[row, LONGITUDES:QUERY_COLS, :] = scaled[0 : TILE // 2]

    n_arrived(across).wait_recv()
    n_out(across).start()

    @pl.loop(1, 4)
    def _(k):
        n_passed(k).start()

    w_own(4).start()

    @pl.loop(1, 4)
    def _(k):
        w_own(k).start()

    project(me)
    n_arrived(chip(1)).wait_recv()
    n_out(chip(1)).start()
    project(across)

    @pl.loop(3, 8)
    def _(j):
        row = chip(j - (1 - j // 5))
        n_arrived(row).wait_recv()
        n_out(row).start()
        project(chip(j - 1 - (1 - (j - 1) // 5)))

        @pl.when(j == 4)
        def _():
            w_arrived(across).wait_recv()
            w_out(across).start()

            @pl.loop(1, 4)
            def _(k):
                w_passed(k).start()

    project(chip(7))

    @pl.loop(1, 4)
    def _(k):
        w_arrived(chip(k)).wait_recv()
        w_out(chip(k)).start()
        w_arrived(chip(k + 4)).wait_recv()
        w_out(chip(k + 4)).start()

    @pl.loop(0, 8)
    def _(k):
        w_in(k).wait_recv()

    made = lax.dot_general(
        up_ref[...], wall[...].reshape(WIDTH, WIDTH), (((1,), (1,)), ((), ())), preferred_element_type=F32
    ).astype(BF)
    for k in range(8):
        ds[k] = made[:, k * 128 : (k + 1) * 128]

    def cotangent(k):
        to = (mp + k) % 16
        return remote(ds.at[to // 2], gb.at[me, own_half], sd.at[k], rd.at[k], {"mp": to})

    def cotangent_in(k):
        by = (mp + 16 - k) % 16
        cut = pl.ds(pl.multiple_of((by % 2) * HALF, HALF), HALF)
        return remote(gb.at[by // 2, cut], gb.at[by // 2, cut], sd.at[k], rd.at[k], {"mp": by})

    @pl.loop(1, 16)
    def _(k):
        cotangent(k).start()

    gb[me, own_half, :] = ds[me]
    u_own(4).start()

    @pl.loop(1, 4)
    def _(k):
        u_own(k).start()

    @pl.loop(1, 16)
    def _(k):
        cotangent_in(k).wait_recv()

    lane = lax.broadcasted_iota(jnp.int32, (LONGITUDES, 128), 1)

    @pl.loop(0, BAND_ROWS)
    def _(row):
        pair = gb[row].astype(F32)
        pair = jnp.where(core == 0, pltpu.roll(pair, HEAD_WIDTH, 1), pair)
        pair = jnp.where(lane < HEAD_WIDTH, 0.0, pair)
        g[row, 0:LONGITUDES, :] = pair
        g[row, LONGITUDES:QUERY_COLS, :] = pair[0 : TILE // 2]

    @pl.loop(0, REACH)
    def _(row):
        up_halo(row + BAND_ROWS - REACH).wait()
        down_halo(row).wait()

    def halo_cut(j):
        return pl.ds(pl.multiple_of(j * 64, 64), 64)

    def down_grad(j):
        cut = halo_cut(j)
        return remote(hs.at[0, :, cut], hr.at[0, :, cut], shg.at[j], rhg.at[j], along(15))

    def up_grad(j):
        cut = halo_cut(j)
        return remote(hs.at[1, :, cut], hr.at[1, :, cut], shg.at[j + 4], rhg.at[j + 4], along(1))

    def leave(j):
        cut = pl.ds(pl.multiple_of(j * 64 + TILE, TILE), 64)
        hs[0, :, halo_cut(j), :] = dkv[0:REACH, cut, :].astype(BF)
        hs[1, :, halo_cut(j), :] = dkv[BAND_ROWS + REACH : KEY_ROWS, cut, :].astype(BF)
        down_grad(j).start()
        up_grad(j).start()

    @pl.loop(0, TILES)
    def _(i):
        attention_tile(i, kv, feat_ref, q, g, pick_ref, live_ref, oq, dkv)

        @pl.when((i % 4 == 0) & (i > 0))
        def _():
            leave(i // 4 - 1)

        @pl.when(i == 8)
        def _():
            u_arrived(across).wait_recv()

            @pl.loop(1, 4)
            def _(k):
                u_passed(k).start()

    dkv[:, LONGITUDES:KEY_COLS, :] += dkv[:, :TILE, :]
    leave(3)
    half = TILE // 2
    oq[:, :half, :] = oq[:, LONGITUDES : LONGITUDES + half, :]
    ab[:, :, 0:128] = oq[:, 0:LONGITUDES, :].astype(BF)
    oq_over = remote(ab.at[:, other_half, 0:128], asib.at[:, :, 0:128], sp.at[1], rp.at[1], sibling)
    oq_over.start()
    weights_over.wait()

    @pl.loop(0, 4)
    def _(j):
        down_grad(j).wait()
        up_grad(j).wait()

    dkv[BAND_ROWS : BAND_ROWS + REACH, TILE:KEY_COLS, :] += hr[0].astype(F32)
    dkv[REACH : 2 * REACH, TILE:KEY_COLS, :] += hr[1].astype(F32)
    ab[:, TILE:LONGITUDES, 128:256] = dkv[REACH : REACH + BAND_ROWS, TILE:LONGITUDES, :].astype(BF)
    ab[:, 0:TILE, 128:256] = dkv[REACH : REACH + BAND_ROWS, LONGITUDES:KEY_COLS, :].astype(BF)
    kv_over = remote(ab.at[:, other_half, 128:256], asib.at[:, :, 128:256], sp.at[2], rp.at[2], sibling)
    kv_over.start()
    oq_over.wait()
    kv_over.wait()

    def grad_part(row):
        both = jnp.concatenate([ab[row, own_half, :], asib[row]], axis=1)
        return jnp.dot(both, wp[...], preferred_element_type=F32)

    def grad_sent(k):
        row = chip(k)
        return remote(gs.at[row], gr.at[k // 4 * 4 + x], sgn.at[k], rgn.at[k // 4 * 4 + x], peer(chip(k % 4)))

    def grad_received(k):
        slot = k // 4 * 4 + chip(k) % 4
        return remote(gr.at[slot], gr.at[slot], sgn.at[k], rgn.at[slot], peer(chip(k % 4)))

    @pl.loop(1, 8)
    def _(j):
        k = (j + 4) % 8

        @pl.when(k % 4 > 0)
        def _():
            gs[chip(k)] = grad_part(chip(k)).astype(BF)
            grad_sent(k).start()

    mine[0] = grad_part(me)
    mine[1] = grad_part(across)

    low = lax.broadcasted_iota(jnp.int32, (HALF, 128), 1) < HEAD_WIDTH

    @pl.loop(0, BAND_ROWS)
    def _(row):
        ours = ab[row, own_half, 0:128].astype(F32)
        theirs = asib[row, :, 0:128].astype(F32)
        first = jnp.where(core == 0, ours, theirs)
        second = jnp.where(core == 0, theirs, ours)
        os[row] = jnp.where(low, pltpu.roll(first, HEAD_WIDTH, 1), second).astype(BF)

    def heads_sent(k):
        return remote(os.at[chip(k)], oa.at[me], so.at[k], ro.at[me], peer(chip(k)))

    def heads_received(row):
        return remote(oa.at[row], oa.at[row], so.at[0], ro.at[row], peer(row))

    @pl.loop(1, 8)
    def _(k):
        heads_sent(k).start()

    oa[me] = os[me]

    @pl.loop(1, 4)
    def _(k):
        u_arrived(chip(k)).wait_recv()
        u_arrived(chip(k + 4)).wait_recv()

    columns = 512

    @pl.loop(0, WIDTH // columns)
    def _(n):
        cut = pl.ds(pl.multiple_of(n * columns, columns), columns)
        part = lax.dot_general(
            os[...].reshape(BAND_ROWS * HALF, 128),
            ub[:, :, cut].reshape(BAND_ROWS * HALF, columns),
            (((0,), (0,)), ((), ())),
            preferred_element_type=F32,
        )
        wx[0:2, :, cut] = part.reshape(2, HEAD_WIDTH, columns)

    out_over = remote(wx.at[1 - core], wx.at[2], sp.at[3], rp.at[3], sibling)
    out_over.start()

    @pl.loop(0, WIDTH // columns)
    def _(n):
        cut = pl.ds(pl.multiple_of(n * columns, columns), columns)
        part = lax.dot_general(
            ab[...].reshape(BAND_ROWS * LONGITUDES, 256),
            nb[:, :, cut].reshape(BAND_ROWS * LONGITUDES, columns),
            (((0,), (0,)), ((), ())),
            preferred_element_type=F32,
        )
        wg[0:64, cut] = part[0:64]
        wg[64:192, cut] = part[128:256]

    out_over.wait()
    wg[192:256, :] = wx[core] + wx[2]
    wgb[...] = wg[...].astype(BF)

    def share(row):
        return pl.ds(pl.multiple_of(row * 16, 16), 16)

    def scatter(k):
        to = (lat + k) % 16
        return remote(wgb.at[share(to)], lr.at[k], sl.at[k], rl.at[k], along(k))

    def gather(k):
        return remote(lf.at[share(lat)], lf.at[share(lat)], sf.at[k], rf.at[k], along(k))

    def gathered(k):
        row = (lat + 16 - k) % 16
        return remote(lf.at[share(row)], lf.at[share(row)], sf.at[k], rf.at[k], along(k))

    @pl.loop(1, 16)
    def _(k):
        scatter(k).start()

    @pl.loop(1, 8)
    def _(k):
        heads_received(chip(k)).wait_recv()

    heads = jnp.concatenate([oa[k] for k in range(8)], axis=1)
    update_ref[...] = jnp.dot(
        heads, wall[...].reshape(WIDTH, WIDTH), preferred_element_type=F32
    ).astype(BF)

    total = mine[1]
    for k in range(5, 8):
        grad_received(k).wait_recv()
        total = total + gr[4 + chip(k) % 4].astype(F32)
    gy[0] = total.astype(BF)
    over_y = remote(gy.at[0], gy.at[1], sp.at[4], rp.at[4], peer(across))
    over_y.start()

    total = wg[share(lat), :]
    for k in range(1, 16):
        scatter(k).wait()
        total = total + lr[k].astype(F32)
    lf[share(lat), :] = (total * (4.0 / math.sqrt(BAND_ROWS * LONGITUDES * 16))).astype(BF)

    @pl.loop(1, 16)
    def _(k):
        gather(k).start()

    total = mine[0]
    for k in range(1, 4):
        grad_received(k).wait_recv()
        total = total + gr[chip(k) % 4].astype(F32)
    over_y.wait()
    total = total + gy[1].astype(F32)
    features, inverse = normalised()
    centred = features * inverse
    scaled = gain_ref[...] * total
    grad_in_ref[...] = (
        inverse * (scaled - centred * jnp.mean(scaled * centred, axis=1, keepdims=True))
    ).astype(BF)

    @pl.loop(1, 16)
    def _(k):
        gather(k).wait_send()
        gathered(k).wait_recv()
        cotangent(k).wait_send()

    grad_qkv_ref[...] = lf[0:192, :].astype(F32)
    grad_out_ref[...] = lf[192:256, :].astype(F32)

    @pl.loop(1, 4)
    def _(k):
        n_own(k).wait_send()
        n_passed(k).wait_send()
        w_own(k).wait_send()
        w_passed(k).wait_send()
        u_own(k).wait_send()
        u_passed(k).wait_send()
        grad_sent(k).wait_send()
        grad_sent(k + 4).wait_send()

    n_own(4).wait_send()
    w_own(4).wait_send()
    u_own(4).wait_send()

    @pl.loop(1, 8)
    def _(k):
        heads_sent(k).wait_send()

    @pl.loop(0, 8)
    def _(k):
        n_out(k).wait_send()
        w_out(k).wait_send()


def on_device(tokens, gain, qkv_weight, out_weight, row_cells, upstream):
    band_start = lax.axis_index("lat") * BAND_ROWS
    cells = lax.dynamic_slice_in_dim(jnp.pad(row_cells, (REACH, REACH)), band_start, KEY_ROWS)
    queries = (BAND_ROWS, QUERY_COLS, 128)
    keys = (KEY_ROWS, KEY_COLS, 128)
    halo = (2, REACH, LONGITUDES, 128)
    wide = (8, HALF, WIDTH)
    pairs = (8, HALF, 128)
    update, grad_input, grad_qkv, grad_out = pl.pallas_call(
        sublayer_kernel,
        out_shape=(
            jax.ShapeDtypeStruct((HALF, WIDTH), BF),
            jax.ShapeDtypeStruct((HALF, WIDTH), BF),
            jax.ShapeDtypeStruct((3 * HEAD_WIDTH, WIDTH), F32),
            jax.ShapeDtypeStruct((HEAD_WIDTH, WIDTH), F32),
        ),
        in_specs=[pl.BlockSpec(memory_space=VMEM)] * 8,
        out_specs=[pl.BlockSpec(memory_space=VMEM)] * 4,
        scratch_shapes=[
            VMEM((BAND_ROWS, LONGITUDES, WIDTH), BF),
            VMEM(wide, BF),
            VMEM((512, WIDTH), BF),
            VMEM((8, 128, WIDTH), BF),
            VMEM(keys, BF),
            VMEM(queries, F32),
            VMEM(queries, F32),
            VMEM(queries, F32),
            VMEM(keys, F32),
            VMEM(halo, BF),
            VMEM(halo, BF),
            VMEM((BAND_ROWS, LONGITUDES, 256), BF),
            VMEM((BAND_ROWS, HALF, 256), BF),
            VMEM(pairs, BF),
            VMEM((BAND_ROWS, LONGITUDES, 128), BF),
            VMEM(pairs, BF),
            VMEM(pairs, BF),
            VMEM(wide, BF),
            VMEM(wide, BF),
            VMEM((2, HALF, WIDTH), BF),
            VMEM((2, HALF, WIDTH), F32),
            VMEM((256, WIDTH), F32),
            VMEM((256, WIDTH), BF),
            VMEM((3, HEAD_WIDTH, WIDTH), F32),
            VMEM((16, 16, WIDTH), BF),
            VMEM((256, WIDTH), BF),
        ]
        + [DMA((8,))] * 20
        + [DMA((16,))] * 6
        + [DMA((5,))] * 2,
        compiler_params=pltpu.CompilerParams(
            collective_id=0, has_side_effects=True, vmem_limit_bytes=56 << 20
        ),
        name="sublayer",
    )(
        tokens,
        gain.reshape(1, WIDTH),
        qkv_weight.reshape(3 * HEAD_WIDTH, WIDTH),
        out_weight.reshape(HEAD_WIDTH, WIDTH),
        upstream,
        key_features(cells),
        query_features(),
        live_queries(cells),
    )
    return (
        update,
        grad_input,
        grad_qkv.reshape(1, 3 * HEAD_WIDTH, WIDTH),
        grad_out.reshape(1, HEAD_WIDTH, WIDTH),
    )


def solution(mesh):
    return jax.shard_map(
        on_device,
        mesh=mesh,
        in_specs=(
            P(("lat", "mp"), None),
            P(),
            P("mp", None, None),
            P("mp", None, None),
            P(),
            P(("lat", "mp"), None),
        ),
        out_specs=(
            P(("lat", "mp"), None),
            P(("lat", "mp"), None),
            P("mp", None, None),
            P("mp", None, None),
        ),
        check_vma=False,
    )
```

```python
import math

import jax
import jax.numpy as jnp
from jax import lax
from jax.experimental import pallas as pl
from jax.experimental.pallas import tpu as pltpu
from jax.sharding import PartitionSpec as P

WIDTH = 1024
HEAD_WIDTH = 64
LONGITUDES = 256
BAND_ROWS = 8
REACH = 6
KEY_ROWS = BAND_ROWS + 2 * REACH
TILE = 16
WINDOW = 2 * TILE
TILES = LONGITUDES // TILE
KEY_COLS = LONGITUDES + TILE
QUERY_COLS = LONGITUDES + TILE // 2
NEVER = -1e30
VMEM = pltpu.VMEM
MESH = pl.DeviceIdType.MESH
HALF = LONGITUDES // 2
BF = jnp.bfloat16
F32 = jnp.float32
DMA = pltpu.SemaphoreType.DMA


def row_features(row, cells):
    shape = (KEY_COLS, 128)
    col = lax.broadcasted_iota(jnp.int32, shape, 0)
    lane = lax.broadcasted_iota(jnp.int32, shape, 1)
    live = (col & (LONGITUDES - 1)) < cells
    near_row = (row >= lane - 8) & (row <= lane - 8 + 2 * REACH)
    apart = (col - lane) & 31
    near_col = (apart <= REACH) | (apart >= 32 - REACH)
    barred = (
        ((lane == 0) & ~live)
        | ((lane >= 8) & (lane < 16) & ~near_row)
        | ((lane >= 32) & (lane < 64) & ~near_col)
    )
    return jnp.where(barred, NEVER, 0.0).astype(BF)


def query_features(parity):
    shape = (BAND_ROWS, TILE, 128)
    row, col, lane = (lax.broadcasted_iota(jnp.int32, shape, d) for d in range(3))
    picked = (
        (lane == 0)
        | (lane == 8 + row)
        | (lane == 32 + ((TILE * parity + TILE // 2 + col) & 31))
    )
    return jnp.where(picked, 1.0, 0.0).reshape(BAND_ROWS * TILE, 128).astype(BF)


def attention_tile(i, kv_ref, feat_ref, q_ref, g_ref, pick_ref, cells, oq_ref, dkv_ref):
    queries = BAND_ROWS * TILE
    keys = KEY_ROWS * WINDOW
    c0 = pl.multiple_of(i * TILE, TILE)
    at = pl.multiple_of(i * TILE + TILE // 2, TILE // 2)
    kv = kv_ref[:, pl.ds(c0, WINDOW), :].reshape(keys, 128)
    feat = feat_ref[:, pl.ds(c0, WINDOW), :].reshape(keys, 128)
    q = q_ref[:, pl.ds(at, TILE), :].reshape(queries, 128).astype(jnp.bfloat16)
    g = g_ref[:, pl.ds(at, TILE), :].reshape(queries, 128).astype(jnp.bfloat16)
    pick = pick_ref[lax.rem(i, 2)]
    both = jnp.concatenate(
        [
            jnp.concatenate([q, pick], axis=1),
            jnp.concatenate([g, jnp.zeros_like(g)], axis=1),
        ],
        axis=0,
    )
    products = lax.dot_general(
        jnp.concatenate([kv, feat], axis=1),
        both,
        (((1,), (1,)), ((), ())),
        preferred_element_type=jnp.float32,
    )
    scores = products[:, :queries]
    grad_probs = products[:, queries:]
    highest = jnp.max(scores, axis=0, keepdims=True)
    terms = jnp.exp(scores - highest)
    query = lax.broadcasted_iota(jnp.int32, (1, queries), 1)
    col = (i * TILE + TILE // 2 + (query & (TILE - 1))) & (LONGITUDES - 1)
    live = jnp.where(col < cells, 1.0, 0.0)
    probs = terms * (live / jnp.sum(terms, axis=0, keepdims=True))
    weights = probs.astype(jnp.bfloat16)
    row_delta = jnp.sum(probs * grad_probs, axis=0, keepdims=True)
    grad_scores = (probs * (grad_probs - row_delta)).astype(jnp.bfloat16)
    pair = jnp.concatenate([weights, grad_scores], axis=1)
    dkv = jnp.dot(pair, jnp.concatenate([g, q], axis=0), preferred_element_type=jnp.float32)
    dkv_ref[:, pl.ds(c0, WINDOW), :] += dkv.reshape(KEY_ROWS, WINDOW, 128)
    out = lax.dot_general(
        pair, kv, (((0,), (0,)), ((), ())), preferred_element_type=jnp.float32
    )
    lane = lax.broadcasted_iota(jnp.int32, (queries, 128), 1)
    oq = jnp.where(lane < HEAD_WIDTH, out[queries:] * (1.0 / math.sqrt(HEAD_WIDTH)), out[:queries])
    oq_ref[:, pl.ds(at, TILE), :] = oq.reshape(BAND_ROWS, TILE, 128)


def remote(src, dst, send_sem, recv_sem, device):
    return pltpu.make_async_remote_copy(
        src_ref=src,
        dst_ref=dst,
        send_sem=send_sem,
        recv_sem=recv_sem,
        device_id=device,
        device_id_type=MESH,
    )


def sublayer_kernel(
    tok_ref, gain_ref, w_ref, wo_ref, up_ref, cells_ref,
    update_ref, grad_in_ref, grads_ref,
    feat, pick, nb, ub, wp, wall, kv, q, g, oq, dkv, hs, hr, ab, asib, ds, gb, os, oa, gs, gr, gy, mine, wg, wgb, wx, lr, lf,
    sn, rn, snf, rnf, su, ru, sw, rw, swf, rwf, sku, rku, skd, rkd, shg, rhg, so, ro, sgn, rgn,
    sd, rd, sl, rl, sf, rf, sp, rp,
):
    lat, mp = lax.axis_index("lat"), lax.axis_index("mp")
    y, x, core = mp // 8, (mp // 2) % 4, mp % 2
    me = mp // 2
    across = (1 - y) * 4 + x
    sibling = {"mp": me * 2 + (1 - core)}

    def halves(width):
        return (
            pl.ds(pl.multiple_of(core * width, width), width),
            pl.ds(pl.multiple_of((1 - core) * width, width), width),
        )

    own_half, other_half = halves(HALF)
    own_head, other_head = halves(HEAD_WIDTH)

    def chip(k):
        d = k % 4
        d = d + (d // 2) * (1 - 2 * (d % 2))
        return ((y + k // 4) % 2) * 4 + (x + d) % 4

    def peer(row):
        return {"mp": row * 2 + core}

    def along(step):
        return {"lat": (lat + step) % 16}

    barrier = pltpu.get_barrier_semaphore()

    @pl.loop(1, 16)
    def _(k):
        pl.semaphore_signal(barrier, inc=1, device_id={"mp": (mp + k) % 16}, device_id_type=MESH)
        pl.semaphore_signal(barrier, inc=1, device_id=along(k), device_id_type=MESH)

    def normalised():
        features = tok_ref[...].astype(F32)
        inverse = lax.rsqrt(jnp.mean(features * features, axis=1, keepdims=True) + 1e-06)
        return features, inverse

    features, inverse = normalised()
    nb[me, own_half, :] = (features * inverse * gain_ref[...]).astype(BF)
    ub[me] = up_ref[...]
    wall[me, own_head, :] = wo_ref[...]
    wp[0:64, :] = w_ref[0:64, :]
    wp[64:128, :] = jnp.zeros((64, WIDTH), BF)
    wp[128:256, :] = w_ref[64:192, :]
    pl.semaphore_wait(barrier, 30)

    east, west, opposite = chip(1), chip(2), chip(3)
    across_east, across_west, across_opposite = chip(5), chip(6), chip(7)

    class Gather:
        def __init__(self, buf, cut, s, r):
            self.at = lambda row: buf.at[row] if cut is None else buf.at[row, cut]
            self.s, self.r = s, r

        def move(self, i):
            block = (me, me, me, across, across, west, across_east)[i]
            to = (across, east, west, east, west, east, west)[i]
            return remote(self.at(block), self.at(block), self.s.at[i], self.r.at[block], peer(to))

        def arrive(self, row):
            remote(self.at(row), self.at(row), self.s.at[0], self.r.at[row], peer(row)).wait_recv()

    def handing(buf, cut, cut_in, s, r):
        def out(row):
            return remote(buf.at[row, cut], buf.at[row, cut], s.at[row], r.at[row], sibling)

        def into(row):
            return remote(buf.at[row, cut_in], buf.at[row, cut_in], s.at[row], r.at[row], sibling)

        return out, into

    n_gather = Gather(nb, own_half, sn, rn)
    n_out, n_in = handing(nb, own_half, other_half, snf, rnf)
    w_gather = Gather(wall, own_head, sw, rw)
    w_out, w_in = handing(wall, own_head, other_head, swf, rwf)
    u_gather = Gather(ub, None, su, ru)

    for i in range(3):
        w_gather.move(i).start()
    for i in range(3):
        n_gather.move(i).start()
    u_gather.move(0).start()
    w_out(me).start()
    n_out(me).start()
    weights_over = remote(wp.at[0:256], wp.at[256:512], sp.at[0], rp.at[0], sibling)
    weights_over.start()

    def cells_of(row):
        inside = (row >= 0) & (row < 128)
        return jnp.where(inside, cells_ref[jnp.clip(row, 0, 127)], 0)

    dkv[...] = jnp.zeros_like(dkv)

    @pl.loop(0, KEY_ROWS)
    def _(row):
        feat[row] = row_features(row, cells_of(lat * BAND_ROWS + row - REACH))

    pick[0] = query_features(0)
    pick[1] = query_features(1)
    query_row = lax.broadcasted_iota(jnp.int32, (1, BAND_ROWS * TILE), 1) // TILE
    query_cells = jnp.zeros((1, BAND_ROWS * TILE), jnp.int32)
    for r in range(BAND_ROWS):
        query_cells = jnp.where(query_row == r, cells_of(lat * BAND_ROWS + r), query_cells)

    def up_halo(row):
        return remote(kv.at[REACH + row], kv.at[row + REACH - BAND_ROWS], sku.at[row], rku.at[row], along(1))

    def down_halo(row):
        return remote(kv.at[REACH + row], kv.at[row + REACH + BAND_ROWS], skd.at[row], rkd.at[row], along(15))

    def project(row):
        n_in(row).wait_recv()
        made = lax.dot_general(
            nb[row], wp[0:256, :], (((1,), (1,)), ((), ())), preferred_element_type=F32
        ).astype(BF)
        kv[REACH + row, 0:LONGITUDES, :] = made[:, 128:256]
        kv[REACH + row, LONGITUDES:KEY_COLS, :] = made[0:TILE, 128:256]

        @pl.when(row >= BAND_ROWS - REACH)
        def _():
            up_halo(row).start()

        @pl.when(row < REACH)
        def _():
            down_halo(row).start()

        scaled = made[:, 0:128].astype(F32) * (1.0 / math.sqrt(HEAD_WIDTH))
        q[row, 0:LONGITUDES, :] = scaled
        q[row, LONGITUDES:QUERY_COLS, :] = scaled[0 : TILE // 2]

    def passed_on(gather, out, row, moves):
        gather.arrive(row)
        for i in moves:
            gather.move(i).start()
        out(row).start()

    passed_on(w_gather, w_out, west, (5,))
    passed_on(w_gather, w_out, across, (3, 4))
    passed_on(n_gather, n_out, west, (5,))
    passed_on(n_gather, n_out, across, (3, 4))
    passed_on(w_gather, w_out, across_east, (6,))
    project(me)
    for row in (east, across_west, opposite, across_opposite):
        passed_on(w_gather, w_out, row, ())
    passed_on(n_gather, n_out, across_east, (6,))
    passed_on(n_gather, n_out, east, ())

    @pl.loop(0, 8)
    def _(k):
        w_in(k).wait_recv()

    made = lax.dot_general(
        up_ref[...], wall[...].reshape(WIDTH, WIDTH), (((1,), (1,)), ((), ())), preferred_element_type=F32
    ).astype(BF)
    for k in range(8):
        ds[k] = made[:, k * 128 : (k + 1) * 128]

    def cotangent(k):
        to = (mp + k) % 16
        return remote(ds.at[to // 2], gb.at[me, own_half], sd.at[k], rd.at[k], {"mp": to})

    def cotangent_in(k):
        by = (mp + 16 - k) % 16
        cut = pl.ds(pl.multiple_of((by % 2) * HALF, HALF), HALF)
        return remote(gb.at[by // 2, cut], gb.at[by // 2, cut], sd.at[k], rd.at[k], {"mp": by})

    @pl.loop(1, 16)
    def _(k):
        cotangent(k).start()

    gb[me, own_half, :] = ds[me]

    @pl.loop(0, 7)
    def _(j):
        k = jnp.where(j == 0, 2, jnp.where(j == 1, 4, jnp.where(j == 2, 1, jnp.where(j == 3, 5, 0))))
        k = jnp.where(j == 4, 3, jnp.where(j == 5, 6, jnp.where(j == 6, 7, k)))

        @pl.when(j < 3)
        def _():
            later = jnp.where(j == 0, 3, jnp.where(j == 1, 6, 7))
            n_gather.arrive(chip(later))
            n_out(chip(later)).start()

        project(chip(k))

    u_gather.arrive(across)
    for i in (1, 2, 3, 4):
        u_gather.move(i).start()

    @pl.loop(1, 16)
    def _(k):
        cotangent_in(k).wait_recv()

    lane = lax.broadcasted_iota(jnp.int32, (LONGITUDES, 128), 1)

    @pl.loop(0, BAND_ROWS)
    def _(row):
        pair = gb[row].astype(F32)
        pair = jnp.where(core == 0, pltpu.roll(pair, HEAD_WIDTH, 1), pair)
        pair = jnp.where(lane < HEAD_WIDTH, 0.0, pair)
        g[row, 0:LONGITUDES, :] = pair
        g[row, LONGITUDES:QUERY_COLS, :] = pair[0 : TILE // 2]

    @pl.loop(0, REACH)
    def _(row):
        up_halo(row + BAND_ROWS - REACH).wait()
        down_halo(row).wait()

    def halo_cut(j):
        return pl.ds(pl.multiple_of(j * 64, 64), 64)

    def down_grad(j):
        cut = halo_cut(j)
        return remote(hs.at[0, :, cut], hr.at[0, :, cut], shg.at[j], rhg.at[j], along(15))

    def up_grad(j):
        cut = halo_cut(j)
        return remote(hs.at[1, :, cut], hr.at[1, :, cut], shg.at[j + 4], rhg.at[j + 4], along(1))

    def leave(j):
        cut = pl.ds(pl.multiple_of(j * 64 + TILE, TILE), 64)
        hs[0, :, halo_cut(j), :] = dkv[0:REACH, cut, :].astype(BF)
        hs[1, :, halo_cut(j), :] = dkv[BAND_ROWS + REACH : KEY_ROWS, cut, :].astype(BF)
        down_grad(j).start()
        up_grad(j).start()

    @pl.loop(0, TILES)
    def _(i):
        attention_tile(i, kv, feat, q, g, pick, query_cells, oq, dkv)

        @pl.when((i % 4 == 0) & (i > 0))
        def _():
            leave(i // 4 - 1)

        @pl.when(i == 10)
        def _():
            u_gather.arrive(west)
            u_gather.move(5).start()
            u_gather.arrive(across_east)
            u_gather.move(6).start()

    dkv[:, LONGITUDES:KEY_COLS, :] += dkv[:, :TILE, :]
    leave(3)
    half = TILE // 2
    oq[:, :half, :] = oq[:, LONGITUDES : LONGITUDES + half, :]
    ab[:, :, 0:128] = oq[:, 0:LONGITUDES, :].astype(BF)
    oq_over = remote(ab.at[:, other_half, 0:128], asib.at[:, :, 0:128], sp.at[1], rp.at[1], sibling)
    oq_over.start()
    weights_over.wait()

    @pl.loop(0, 4)
    def _(j):
        down_grad(j).wait()
        up_grad(j).wait()

    dkv[BAND_ROWS : BAND_ROWS + REACH, TILE:KEY_COLS, :] += hr[0].astype(F32)
    dkv[REACH : 2 * REACH, TILE:KEY_COLS, :] += hr[1].astype(F32)
    ab[:, TILE:LONGITUDES, 128:256] = dkv[REACH : REACH + BAND_ROWS, TILE:LONGITUDES, :].astype(BF)
    ab[:, 0:TILE, 128:256] = dkv[REACH : REACH + BAND_ROWS, LONGITUDES:KEY_COLS, :].astype(BF)
    kv_over = remote(ab.at[:, other_half, 128:256], asib.at[:, :, 128:256], sp.at[2], rp.at[2], sibling)
    kv_over.start()
    oq_over.wait()
    kv_over.wait()

    def grad_part(row):
        both = jnp.concatenate([ab[row, own_half, :], asib[row]], axis=1)
        return jnp.dot(both, wp[...], preferred_element_type=F32)

    def grad_sent(i):
        to = (east, west, west, east, east, west)[i]
        return remote(gs.at[i], gr.at[i], sgn.at[i], rgn.at[i], peer(to))

    gs[1] = grad_part(across_opposite).astype(BF)
    grad_sent(1).start()
    gs[0] = grad_part(opposite).astype(BF)
    grad_sent(0).start()

    low = lax.broadcasted_iota(jnp.int32, (HALF, 128), 1) < HEAD_WIDTH

    @pl.loop(0, BAND_ROWS)
    def _(row):
        ours = ab[row, own_half, 0:128].astype(F32)
        theirs = asib[row, :, 0:128].astype(F32)
        first = jnp.where(core == 0, ours, theirs)
        second = jnp.where(core == 0, theirs, ours)
        os[row] = jnp.where(low, pltpu.roll(first, HEAD_WIDTH, 1), second).astype(BF)

    def heads_sent(k):
        return remote(os.at[chip(k)], oa.at[me], so.at[k], ro.at[me], peer(chip(k)))

    def heads_received(row):
        return remote(oa.at[row], oa.at[row], so.at[0], ro.at[row], peer(row))

    @pl.loop(1, 8)
    def _(k):
        heads_sent(k).start()

    oa[me] = os[me]

    for row in (east, across_west, opposite, across_opposite):
        u_gather.arrive(row)

    columns = 512

    @pl.loop(0, WIDTH // columns)
    def _(n):
        cut = pl.ds(pl.multiple_of(n * columns, columns), columns)
        part = lax.dot_general(
            os[...].reshape(BAND_ROWS * HALF, 128),
            ub[:, :, cut].reshape(BAND_ROWS * HALF, columns),
            (((0,), (0,)), ((), ())),
            preferred_element_type=F32,
        )
        wx[0:2, :, cut] = part.reshape(2, HEAD_WIDTH, columns)

    out_over = remote(wx.at[1 - core], wx.at[2], sp.at[3], rp.at[3], sibling)
    out_over.start()

    @pl.loop(0, WIDTH // columns)
    def _(n):
        cut = pl.ds(pl.multiple_of(n * columns, columns), columns)
        part = lax.dot_general(
            ab[...].reshape(BAND_ROWS * LONGITUDES, 256),
            nb[:, :, cut].reshape(BAND_ROWS * LONGITUDES, columns),
            (((0,), (0,)), ((), ())),
            preferred_element_type=F32,
        )
        wg[0:64, cut] = part[0:64]
        wg[64:192, cut] = part[128:256]

    out_over.wait()
    wg[192:256, :] = wx[core] + wx[2]
    wgb[...] = wg[...].astype(BF)

    def share(row):
        return pl.ds(pl.multiple_of(row * 16, 16), 16)

    def scatter(k):
        to = (lat + k) % 16
        return remote(wgb.at[share(to)], lr.at[k], sl.at[k], rl.at[k], along(k))

    def gather(k):
        return remote(lf.at[share(lat)], lf.at[share(lat)], sf.at[k], rf.at[k], along(k))

    def gathered(k):
        row = (lat + 16 - k) % 16
        return remote(lf.at[share(row)], lf.at[share(row)], sf.at[k], rf.at[k], along(k))

    @pl.loop(1, 16)
    def _(k):
        scatter(k).start()

    grad_sent(1).wait_recv()
    gs[2] = (grad_part(across_west) + gr[1].astype(F32)).astype(BF)
    grad_sent(2).start()
    gs[3] = grad_part(across_east).astype(BF)
    grad_sent(3).start()
    grad_sent(0).wait_recv()
    gs[4] = (grad_part(east) + gr[0].astype(F32)).astype(BF)
    grad_sent(4).start()
    gs[5] = grad_part(west).astype(BF)
    grad_sent(5).start()
    mine[0] = grad_part(me)
    mine[1] = grad_part(across)
    grad_sent(2).wait_recv()
    grad_sent(3).wait_recv()
    gy[0] = (mine[1] + gr[2].astype(F32) + gr[3].astype(F32)).astype(BF)
    over_y = remote(gy.at[0], gy.at[1], sp.at[4], rp.at[4], peer(across))
    over_y.start()

    @pl.loop(1, 8)
    def _(k):
        heads_received(chip(k)).wait_recv()

    heads = jnp.concatenate([oa[k] for k in range(8)], axis=1)
    update_ref[...] = jnp.dot(heads, wall[...].reshape(WIDTH, WIDTH), preferred_element_type=F32)

    total = wg[share(lat), :]
    for k in range(1, 16):
        scatter(k).wait()
        total = total + lr[k].astype(F32)
    lf[share(lat), :] = (total * (4.0 / math.sqrt(BAND_ROWS * LONGITUDES * 16))).astype(BF)

    @pl.loop(1, 16)
    def _(k):
        gather(k).start()

    grad_sent(4).wait_recv()
    grad_sent(5).wait_recv()
    total = mine[0] + gr[4].astype(F32) + gr[5].astype(F32)
    over_y.wait()
    total = total + gy[1].astype(F32)
    features, inverse = normalised()
    centred = features * inverse
    scaled = gain_ref[...] * total
    grad_in_ref[...] = inverse * (
        scaled - centred * jnp.mean(scaled * centred, axis=1, keepdims=True)
    )

    @pl.loop(1, 16)
    def _(k):
        gather(k).wait_send()
        gathered(k).wait_recv()
        cotangent(k).wait_send()

    grads_ref[...] = lf[...]

    for i in range(7):
        n_gather.move(i).wait_send()
        w_gather.move(i).wait_send()
        u_gather.move(i).wait_send()
    for i in range(6):
        grad_sent(i).wait_send()

    @pl.loop(1, 8)
    def _(k):
        heads_sent(k).wait_send()

    @pl.loop(0, 8)
    def _(k):
        n_out(k).wait_send()
        w_out(k).wait_send()


def on_device(tokens, gain, qkv_weight, out_weight, row_cells, upstream):
    queries = (BAND_ROWS, QUERY_COLS, 128)
    keys = (KEY_ROWS, KEY_COLS, 128)
    halo = (2, REACH, LONGITUDES, 128)
    wide = (8, HALF, WIDTH)
    pairs = (8, HALF, 128)
    update, grad_input, grads = pl.pallas_call(
        sublayer_kernel,
        out_shape=(
            jax.ShapeDtypeStruct((HALF, WIDTH), F32),
            jax.ShapeDtypeStruct((HALF, WIDTH), F32),
            jax.ShapeDtypeStruct((256, WIDTH), BF),
        ),
        in_specs=[pl.BlockSpec(memory_space=VMEM)] * 5 + [pl.BlockSpec(memory_space=pltpu.SMEM)],
        out_specs=[pl.BlockSpec(memory_space=VMEM)] * 3,
        scratch_shapes=[
            VMEM(keys, BF),
            VMEM((2, BAND_ROWS * TILE, 128), BF),
            VMEM((BAND_ROWS, LONGITUDES, WIDTH), BF),
            VMEM(wide, BF),
            VMEM((512, WIDTH), BF),
            VMEM((8, 128, WIDTH), BF),
            VMEM(keys, BF),
            VMEM(queries, F32),
            VMEM(queries, F32),
            VMEM(queries, F32),
            VMEM(keys, F32),
            VMEM(halo, BF),
            VMEM(halo, BF),
            VMEM((BAND_ROWS, LONGITUDES, 256), BF),
            VMEM((BAND_ROWS, HALF, 256), BF),
            VMEM(pairs, BF),
            VMEM((BAND_ROWS, LONGITUDES, 128), BF),
            VMEM(pairs, BF),
            VMEM(pairs, BF),
            VMEM(wide, BF),
            VMEM(wide, BF),
            VMEM((2, HALF, WIDTH), BF),
            VMEM((2, HALF, WIDTH), F32),
            VMEM((256, WIDTH), F32),
            VMEM((256, WIDTH), BF),
            VMEM((3, HEAD_WIDTH, WIDTH), F32),
            VMEM((16, 16, WIDTH), BF),
            VMEM((256, WIDTH), BF),
        ]
        + [DMA((8,))] * 20
        + [DMA((16,))] * 6
        + [DMA((5,))] * 2,
        compiler_params=pltpu.CompilerParams(
            collective_id=0, has_side_effects=True, vmem_limit_bytes=56 << 20
        ),
        name="sublayer",
    )(
        tokens,
        gain.reshape(1, WIDTH),
        qkv_weight.reshape(3 * HEAD_WIDTH, WIDTH),
        out_weight.reshape(HEAD_WIDTH, WIDTH),
        upstream,
        row_cells,
    )
    grads = grads.astype(F32)
    return (
        update.astype(BF),
        grad_input.astype(BF),
        grads[0 : 3 * HEAD_WIDTH].reshape(1, 3 * HEAD_WIDTH, WIDTH),
        grads[3 * HEAD_WIDTH :].reshape(1, HEAD_WIDTH, WIDTH),
    )


def solution(mesh):
    return jax.shard_map(
        on_device,
        mesh=mesh,
        in_specs=(
            P(("lat", "mp"), None),
            P(),
            P("mp", None, None),
            P("mp", None, None),
            P(),
            P(("lat", "mp"), None),
        ),
        out_specs=(
            P(("lat", "mp"), None),
            P(("lat", "mp"), None),
            P("mp", None, None),
            P("mp", None, None),
        ),
        check_vma=False,
    )
```

```python
import math

import jax
import jax.numpy as jnp
from jax import lax
from jax.experimental import pallas as pl
from jax.experimental.pallas import tpu as pltpu
from jax.sharding import PartitionSpec as P

WIDTH = 1024
HEAD_WIDTH = 64
LONGITUDES = 256
BAND_ROWS = 8
REACH = 6
KEY_ROWS = BAND_ROWS + 2 * REACH
TILE = 16
WINDOW = 2 * TILE
TILES = LONGITUDES // TILE
KEY_COLS = LONGITUDES + TILE
QUERY_COLS = LONGITUDES + TILE // 2
NEVER = -1e30
VMEM = pltpu.VMEM
MESH = pl.DeviceIdType.MESH
HALF = LONGITUDES // 2
BF = jnp.bfloat16
F32 = jnp.float32
DMA = pltpu.SemaphoreType.DMA


def row_features(row, cells):
    shape = (KEY_COLS, 128)
    col = lax.broadcasted_iota(jnp.int32, shape, 0)
    lane = lax.broadcasted_iota(jnp.int32, shape, 1)
    live = (col & (LONGITUDES - 1)) < cells
    near_row = (row >= lane - 8) & (row <= lane - 8 + 2 * REACH)
    apart = (col - lane) & 31
    near_col = (apart <= REACH) | (apart >= 32 - REACH)
    barred = (
        ((lane == 0) & ~live)
        | ((lane >= 8) & (lane < 16) & ~near_row)
        | ((lane >= 32) & (lane < 64) & ~near_col)
    )
    return jnp.where(barred, NEVER, 0.0).astype(BF)


def query_features(parity):
    shape = (BAND_ROWS, TILE, 128)
    row, col, lane = (lax.broadcasted_iota(jnp.int32, shape, d) for d in range(3))
    picked = (
        (lane == 0)
        | (lane == 8 + row)
        | (lane == 32 + ((TILE * parity + TILE // 2 + col) & 31))
    )
    return jnp.where(picked, 1.0, 0.0).reshape(BAND_ROWS * TILE, 128).astype(BF)


def attention_tile(i, kv_ref, feat_ref, q_ref, g_ref, pick_ref, cells, oq_ref, dkv_ref):
    queries = BAND_ROWS * TILE
    keys = KEY_ROWS * WINDOW
    c0 = pl.multiple_of(i * TILE, TILE)
    at = pl.multiple_of(i * TILE + TILE // 2, TILE // 2)
    kv = kv_ref[:, pl.ds(c0, WINDOW), :].reshape(keys, 128)
    feat = feat_ref[:, pl.ds(c0, WINDOW), :].reshape(keys, 128)
    q = q_ref[:, pl.ds(at, TILE), :].reshape(queries, 128).astype(jnp.bfloat16)
    g = g_ref[:, pl.ds(at, TILE), :].reshape(queries, 128).astype(jnp.bfloat16)
    pick = pick_ref[lax.rem(i, 2)]
    both = jnp.concatenate(
        [
            jnp.concatenate([q, pick], axis=1),
            jnp.concatenate([g, jnp.zeros_like(g)], axis=1),
        ],
        axis=0,
    )
    products = lax.dot_general(
        jnp.concatenate([kv, feat], axis=1),
        both,
        (((1,), (1,)), ((), ())),
        preferred_element_type=jnp.float32,
    )
    scores = products[:, :queries]
    grad_probs = products[:, queries:]
    highest = jnp.max(scores, axis=0, keepdims=True)
    terms = jnp.exp(scores - highest)
    query = lax.broadcasted_iota(jnp.int32, (1, queries), 1)
    col = (i * TILE + TILE // 2 + (query & (TILE - 1))) & (LONGITUDES - 1)
    live = jnp.where(col < cells, 1.0, 0.0)
    probs = terms * (live / jnp.sum(terms, axis=0, keepdims=True))
    weights = probs.astype(jnp.bfloat16)
    row_delta = jnp.sum(probs * grad_probs, axis=0, keepdims=True)
    grad_scores = (probs * (grad_probs - row_delta)).astype(jnp.bfloat16)
    pair = jnp.concatenate([weights, grad_scores], axis=1)
    dkv = jnp.dot(pair, jnp.concatenate([g, q], axis=0), preferred_element_type=jnp.float32)
    dkv_ref[:, pl.ds(c0, WINDOW), :] += dkv.reshape(KEY_ROWS, WINDOW, 128)
    out = lax.dot_general(
        pair, kv, (((0,), (0,)), ((), ())), preferred_element_type=jnp.float32
    )
    lane = lax.broadcasted_iota(jnp.int32, (queries, 128), 1)
    oq = jnp.where(lane < HEAD_WIDTH, out[queries:] * (1.0 / math.sqrt(HEAD_WIDTH)), out[:queries])
    oq_ref[:, pl.ds(at, TILE), :] = oq.reshape(BAND_ROWS, TILE, 128)


def remote(src, dst, send_sem, recv_sem, device):
    return pltpu.make_async_remote_copy(
        src_ref=src,
        dst_ref=dst,
        send_sem=send_sem,
        recv_sem=recv_sem,
        device_id=device,
        device_id_type=MESH,
    )


def sublayer_kernel(
    tok_ref, gain_ref, w_ref, wo_ref, up_ref, cells_ref,
    update_ref, grad_in_ref, grads_ref,
    feat, pick, nb, ub, wp, wall, kv, q, g, oq, dkv, hs, hr, ab, asib, ds, gb, os, oa, gs, gr, gy, mine, wg, wgb, wx, lr, lf,
    sn, rn, snf, rnf, su, ru, sw, rw, swf, rwf, sku, rku, skd, rkd, shg, rhg, so, ro, sgn, rgn,
    sd, rd, sl, rl, sf, rf, sp, rp,
):
    lat, mp = lax.axis_index("lat"), lax.axis_index("mp")
    y, x, core = mp // 8, (mp // 2) % 4, mp % 2
    me = mp // 2
    across = (1 - y) * 4 + x
    sibling = {"mp": me * 2 + (1 - core)}

    def halves(width):
        return (
            pl.ds(pl.multiple_of(core * width, width), width),
            pl.ds(pl.multiple_of((1 - core) * width, width), width),
        )

    own_half, other_half = halves(HALF)
    own_head, other_head = halves(HEAD_WIDTH)

    def chip(k):
        d = k % 4
        d = d + (d // 2) * (1 - 2 * (d % 2))
        return ((y + k // 4) % 2) * 4 + (x + d) % 4

    def peer(row):
        return {"mp": row * 2 + core}

    def along(step):
        return {"lat": (lat + step) % 16}

    barrier = pltpu.get_barrier_semaphore()

    @pl.loop(1, 16)
    def _(k):
        pl.semaphore_signal(barrier, inc=1, device_id={"mp": (mp + k) % 16}, device_id_type=MESH)
        pl.semaphore_signal(barrier, inc=1, device_id=along(k), device_id_type=MESH)

    def normalised():
        features = tok_ref[...].astype(F32)
        inverse = lax.rsqrt(jnp.mean(features * features, axis=1, keepdims=True) + 1e-06)
        return features, inverse

    features, inverse = normalised()
    nb[me, own_half, :] = (features * inverse * gain_ref[...]).astype(BF)
    ub[me] = up_ref[...]
    wall[me, own_head, :] = wo_ref[...]
    wp[0:64, :] = w_ref[0:64, :]
    wp[64:128, :] = jnp.zeros((64, WIDTH), BF)
    wp[128:256, :] = w_ref[64:192, :]
    pl.semaphore_wait(barrier, 30)

    east, west, opposite = chip(1), chip(2), chip(3)
    across_east, across_west, across_opposite = chip(5), chip(6), chip(7)

    class Gather:
        def __init__(self, buf, cut, s, r):
            self.at = lambda row: buf.at[row] if cut is None else buf.at[row, cut]
            self.s, self.r = s, r

        def move(self, i):
            block = (me, me, me, across, across, west, across_east)[i]
            to = (across, east, west, east, west, east, west)[i]
            return remote(self.at(block), self.at(block), self.s.at[i], self.r.at[block], peer(to))

        def arrive(self, row):
            remote(self.at(row), self.at(row), self.s.at[0], self.r.at[row], peer(row)).wait_recv()

    def handing(buf, cut, cut_in, s, r):
        def out(row):
            return remote(buf.at[row, cut], buf.at[row, cut], s.at[row], r.at[row], sibling)

        def into(row):
            return remote(buf.at[row, cut_in], buf.at[row, cut_in], s.at[row], r.at[row], sibling)

        return out, into

    n_gather = Gather(nb, own_half, sn, rn)
    n_out, n_in = handing(nb, own_half, other_half, snf, rnf)
    w_gather = Gather(wall, own_head, sw, rw)
    w_out, w_in = handing(wall, own_head, other_head, swf, rwf)
    u_gather = Gather(ub, None, su, ru)

    for i in range(3):
        n_gather.move(i).start()
    n_out(me).start()
    for i in range(3):
        w_gather.move(i).start()
    w_out(me).start()
    weights_over = remote(wp.at[0:256], wp.at[256:512], sp.at[0], rp.at[0], sibling)
    weights_over.start()

    def cells_of(row):
        inside = (row >= 0) & (row < 128)
        return jnp.where(inside, cells_ref[jnp.clip(row, 0, 127)], 0)

    dkv[...] = jnp.zeros_like(dkv)

    @pl.loop(0, KEY_ROWS)
    def _(row):
        feat[row] = row_features(row, cells_of(lat * BAND_ROWS + row - REACH))

    pick[0] = query_features(0)
    pick[1] = query_features(1)
    query_row = lax.broadcasted_iota(jnp.int32, (1, BAND_ROWS * TILE), 1) // TILE
    query_cells = jnp.zeros((1, BAND_ROWS * TILE), jnp.int32)
    for r in range(BAND_ROWS):
        query_cells = jnp.where(query_row == r, cells_of(lat * BAND_ROWS + r), query_cells)

    def whole(row):
        return kv.at[row, 0:LONGITUDES]

    def up_halo(row):
        return remote(whole(REACH + row), whole(row + REACH - BAND_ROWS), sku.at[row], rku.at[row], along(1))

    def down_halo(row):
        return remote(whole(REACH + row), whole(row + REACH + BAND_ROWS), skd.at[row], rkd.at[row], along(15))

    def project(row):
        n_in(row).wait_recv()
        made = lax.dot_general(
            nb[row], wp[0:256, :], (((1,), (1,)), ((), ())), preferred_element_type=F32
        ).astype(BF)
        kv[REACH + row, 0:LONGITUDES, :] = made[:, 128:256]
        kv[REACH + row, LONGITUDES:KEY_COLS, :] = made[0:TILE, 128:256]

        @pl.when(row >= BAND_ROWS - REACH)
        def _():
            up_halo(row).start()

        @pl.when(row < REACH)
        def _():
            down_halo(row).start()

        scaled = made[:, 0:128].astype(F32) * (1.0 / math.sqrt(HEAD_WIDTH))
        q[row, 0:LONGITUDES, :] = scaled
        q[row, LONGITUDES:QUERY_COLS, :] = scaled[0 : TILE // 2]

    def passed_on(gather, out, row, moves):
        gather.arrive(row)
        for i in moves:
            gather.move(i).start()
        out(row).start()

    def cotangent(row, c):
        k = row * 2 + c
        return remote(ds.at[row], gb.at[me, own_half], sd.at[k], rd.at[mp], {"mp": k})

    def cotangent_in(row, c):
        cut = pl.ds(c * HALF, HALF)
        k = row * 2 + c
        return remote(gb.at[row, cut], gb.at[row, cut], sd.at[k], rd.at[k], {"mp": k})

    def cotangents(row):
        w_in(row).wait_recv()
        ds[row] = lax.dot_general(
            up_ref[...], wall[row], (((1,), (1,)), ((), ())), preferred_element_type=F32
        ).astype(BF)
        cotangent(row, 0).start()
        cotangent(row, 1).start()

    project(me)
    passed_on(n_gather, n_out, west, (5,))
    passed_on(n_gather, n_out, across, (3, 4))
    passed_on(w_gather, w_out, west, (5,))
    passed_on(w_gather, w_out, across, (3, 4))
    passed_on(n_gather, n_out, east, ())
    project(west)
    project(across)
    passed_on(n_gather, n_out, across_east, (6,))
    passed_on(w_gather, w_out, across_east, (6,))
    project(east)
    passed_on(n_gather, n_out, opposite, ())
    project(across_east)
    passed_on(n_gather, n_out, across_west, ())
    project(opposite)
    passed_on(w_gather, w_out, east, ())
    passed_on(w_gather, w_out, across_west, ())
    cotangents(west)
    cotangents(across)
    cotangents(across_east)
    passed_on(n_gather, n_out, across_opposite, ())
    project(across_west)
    passed_on(w_gather, w_out, opposite, ())
    passed_on(w_gather, w_out, across_opposite, ())
    cotangents(east)
    cotangents(across_west)
    cotangents(opposite)
    project(across_opposite)
    cotangents(across_opposite)
    w_in(me).wait_recv()
    ds[me] = lax.dot_general(
        up_ref[...], wall[me], (((1,), (1,)), ((), ())), preferred_element_type=F32
    ).astype(BF)
    home = remote(ds.at[me], gb.at[me, own_half], sp.at[5], rp.at[5], sibling)
    home.start()
    gb[me, own_half, :] = ds[me]
    for i in range(3):
        u_gather.move(i).start()

    lane = lax.broadcasted_iota(jnp.int32, (LONGITUDES, 128), 1)

    def cotangent_rows(row):
        pair = gb[row].astype(F32)
        pair = jnp.where(core == 0, pltpu.roll(pair, HEAD_WIDTH, 1), pair)
        pair = jnp.where(lane < HEAD_WIDTH, 0.0, pair)
        g[row, 0:LONGITUDES, :] = pair
        g[row, LONGITUDES:QUERY_COLS, :] = pair[0 : TILE // 2]

    @pl.loop(1, 8)
    def _(k):
        cotangent_in(chip(k), 0).wait_recv()
        cotangent_in(chip(k), 1).wait_recv()
        cotangent_rows(chip(k))

    home.wait()
    cotangent_rows(me)

    @pl.loop(0, REACH)
    def _(row):
        up_halo(row + BAND_ROWS - REACH).wait()
        down_halo(row).wait()

    kv[0:REACH, LONGITUDES:KEY_COLS, :] = kv[0:REACH, 0:TILE, :]
    kv[BAND_ROWS + REACH : KEY_ROWS, LONGITUDES:KEY_COLS, :] = kv[BAND_ROWS + REACH : KEY_ROWS, 0:TILE, :]

    def halo_cut(j):
        return pl.ds(pl.multiple_of(j * WINDOW, WINDOW), WINDOW)

    def down_grad(j):
        cut = halo_cut(j)
        return remote(hs.at[0, :, cut], hr.at[0, :, cut], shg.at[j], rhg.at[j], along(15))

    def up_grad(j):
        cut = halo_cut(j)
        return remote(hs.at[1, :, cut], hr.at[1, :, cut], shg.at[j + 8], rhg.at[j + 8], along(1))

    def leave(j):
        cut = pl.ds(pl.multiple_of(j * WINDOW + TILE, TILE), WINDOW)
        hs[0, :, halo_cut(j), :] = dkv[0:REACH, cut, :].astype(BF)
        hs[1, :, halo_cut(j), :] = dkv[BAND_ROWS + REACH : KEY_ROWS, cut, :].astype(BF)
        down_grad(j).start()
        up_grad(j).start()

    @pl.loop(0, TILES)
    def _(i):
        attention_tile(i, kv, feat, q, g, pick, query_cells, oq, dkv)

        @pl.when((i % 2 == 0) & (i > 0))
        def _():
            leave(i // 2 - 1)

        @pl.when(i == 6)
        def _():
            u_gather.arrive(across)
            u_gather.move(3).start()
            u_gather.move(4).start()

        @pl.when(i == 8)
        def _():
            u_gather.arrive(west)
            u_gather.move(5).start()

        @pl.when(i == 13)
        def _():
            u_gather.arrive(across_east)
            u_gather.move(6).start()

    dkv[:, LONGITUDES:KEY_COLS, :] += dkv[:, :TILE, :]
    leave(7)
    half = TILE // 2
    oq[:, :half, :] = oq[:, LONGITUDES : LONGITUDES + half, :]
    ab[:, :, 0:128] = oq[:, 0:LONGITUDES, :].astype(BF)
    oq_over = remote(ab.at[:, other_half, 0:128], asib.at[:, :, 0:128], sp.at[1], rp.at[1], sibling)
    oq_over.start()

    columns = 512

    @pl.loop(0, WIDTH // columns)
    def _(n):
        cut = pl.ds(pl.multiple_of(n * columns, columns), columns)
        part = lax.dot_general(
            ab[:, :, 0:128].reshape(BAND_ROWS * LONGITUDES, 128),
            nb[:, :, cut].reshape(BAND_ROWS * LONGITUDES, columns),
            (((0,), (0,)), ((), ())),
            preferred_element_type=F32,
        )
        wg[0, 0:64, cut] = part[0:64]

    weights_over.wait()
    oq_over.wait()

    low = lax.broadcasted_iota(jnp.int32, (HALF, 128), 1) < HEAD_WIDTH

    @pl.loop(0, BAND_ROWS)
    def _(row):
        ours = ab[row, own_half, 0:128].astype(F32)
        theirs = asib[row, :, 0:128].astype(F32)
        first = jnp.where(core == 0, ours, theirs)
        second = jnp.where(core == 0, theirs, ours)
        os[row] = jnp.where(low, pltpu.roll(first, HEAD_WIDTH, 1), second).astype(BF)

    def heads_sent(k):
        return remote(os.at[chip(k)], oa.at[me], so.at[k], ro.at[me], peer(chip(k)))

    def heads_received(row):
        return remote(oa.at[row], oa.at[row], so.at[0], ro.at[row], peer(row))

    @pl.loop(1, 8)
    def _(k):
        heads_sent(k).start()

    oa[me] = os[me]

    for row in (east, across_west, opposite, across_opposite):
        u_gather.arrive(row)

    @pl.loop(0, WIDTH // columns)
    def _(n):
        cut = pl.ds(pl.multiple_of(n * columns, columns), columns)
        part = lax.dot_general(
            os[...].reshape(BAND_ROWS * HALF, 128),
            ub[:, :, cut].reshape(BAND_ROWS * HALF, columns),
            (((0,), (0,)), ((), ())),
            preferred_element_type=F32,
        )
        wx[0:2, :, cut] = part.reshape(2, HEAD_WIDTH, columns)

    out_over = remote(wx.at[1 - core], wx.at[2], sp.at[3], rp.at[3], sibling)
    out_over.start()

    @pl.loop(0, 8)
    def _(j):
        down_grad(j).wait()
        up_grad(j).wait()

    dkv[BAND_ROWS : BAND_ROWS + REACH, TILE:KEY_COLS, :] += hr[0].astype(F32)
    dkv[REACH : 2 * REACH, TILE:KEY_COLS, :] += hr[1].astype(F32)
    ab[:, TILE:LONGITUDES, 128:256] = dkv[REACH : REACH + BAND_ROWS, TILE:LONGITUDES, :].astype(BF)
    ab[:, 0:TILE, 128:256] = dkv[REACH : REACH + BAND_ROWS, LONGITUDES:KEY_COLS, :].astype(BF)
    kv_over = remote(ab.at[:, other_half, 128:256], asib.at[:, :, 128:256], sp.at[2], rp.at[2], sibling)
    kv_over.start()

    def share(b):
        rows = pl.ds(pl.multiple_of((b // 2) * 16, 16), 16)
        return rows, pl.ds(pl.multiple_of((b % 2) * columns, columns), columns)

    def scatter(p, k):
        rows, cut = share((lat + k) % 16)
        return remote(wgb.at[p, rows, cut], lr.at[p, k], sl.at[p * 16 + k], rl.at[p * 16 + k], along(k))

    def gather(p, k):
        rows, cut = share(lat)
        return remote(lf.at[p, rows, cut], lf.at[p, rows, cut], sf.at[p * 16 + k], rf.at[p * 16 + k], along(k))

    def gathered(p, k):
        rows, cut = share((lat + 16 - k) % 16)
        return remote(lf.at[p, rows, cut], lf.at[p, rows, cut], sf.at[p * 16 + k], rf.at[p * 16 + k], along(k))

    def scatter_all(p):
        wgb[p] = wg[p].astype(BF)

        @pl.loop(1, 16)
        def _(k):
            scatter(p, k).start()

    def sum_all(p):
        rows, cut = share(lat)
        total = wg[p, rows, cut]
        for k in range(1, 16):
            scatter(p, k).wait()
            total = total + lr[p, k].astype(F32)
        lf[p, rows, cut] = (total * (4.0 / math.sqrt(BAND_ROWS * LONGITUDES * 16))).astype(BF)

        @pl.loop(1, 16)
        def _(k):
            gather(p, k).start()

    out_over.wait()
    wg[0, 64:128, :] = wx[core] + wx[2]
    scatter_all(0)
    kv_over.wait()

    def grad_part(row):
        both = jnp.concatenate([ab[row, own_half, :], asib[row]], axis=1)
        return jnp.dot(both, wp[...], preferred_element_type=F32)

    def grad_sent(i):
        to = (east, west, west, east, east, west)[i]
        return remote(gs.at[i], gr.at[i], sgn.at[i], rgn.at[i], peer(to))

    gs[1] = grad_part(across_opposite).astype(BF)
    grad_sent(1).start()
    gs[0] = grad_part(opposite).astype(BF)
    grad_sent(0).start()
    gs[3] = grad_part(across_east).astype(BF)
    grad_sent(3).start()

    @pl.loop(0, WIDTH // columns)
    def _(n):
        cut = pl.ds(pl.multiple_of(n * columns, columns), columns)
        wg[1, :, cut] = lax.dot_general(
            ab[:, :, 128:256].reshape(BAND_ROWS * LONGITUDES, 128),
            nb[:, :, cut].reshape(BAND_ROWS * LONGITUDES, columns),
            (((0,), (0,)), ((), ())),
            preferred_element_type=F32,
        )

    scatter_all(1)
    mine[1] = grad_part(across_west)
    grad_sent(1).wait_recv()
    gs[2] = (mine[1] + gr[1].astype(F32)).astype(BF)
    grad_sent(2).start()
    mine[0] = grad_part(east)
    grad_sent(0).wait_recv()
    gs[4] = (mine[0] + gr[0].astype(F32)).astype(BF)
    grad_sent(4).start()
    gs[5] = grad_part(west).astype(BF)
    grad_sent(5).start()
    mine[0] = grad_part(me)
    mine[1] = grad_part(across)
    sum_all(0)
    grad_sent(2).wait_recv()
    grad_sent(3).wait_recv()
    gy[0] = (mine[1] + gr[2].astype(F32) + gr[3].astype(F32)).astype(BF)
    over_y = remote(gy.at[0], gy.at[1], sp.at[4], rp.at[4], peer(across))
    over_y.start()
    sum_all(1)

    @pl.loop(1, 8)
    def _(k):
        heads_received(chip(k)).wait_recv()

    heads = jnp.concatenate([oa[k] for k in range(8)], axis=1)
    update_ref[...] = jnp.dot(heads, wall[...].reshape(WIDTH, WIDTH), preferred_element_type=F32)

    grad_sent(4).wait_recv()
    grad_sent(5).wait_recv()
    total = mine[0] + gr[4].astype(F32) + gr[5].astype(F32)
    over_y.wait()
    total = total + gy[1].astype(F32)
    features, inverse = normalised()
    centred = features * inverse
    scaled = gain_ref[...] * total
    grad_in_ref[...] = inverse * (
        scaled - centred * jnp.mean(scaled * centred, axis=1, keepdims=True)
    )

    @pl.loop(1, 16)
    def _(k):
        for p in range(2):
            gather(p, k).wait_send()
            gathered(p, k).wait_recv()

    @pl.loop(1, 8)
    def _(k):
        cotangent(chip(k), 0).wait_send()
        cotangent(chip(k), 1).wait_send()

    grads_ref[...] = lf[...]

    for i in range(7):
        n_gather.move(i).wait_send()
        w_gather.move(i).wait_send()
        u_gather.move(i).wait_send()
    for i in range(6):
        grad_sent(i).wait_send()

    @pl.loop(1, 8)
    def _(k):
        heads_sent(k).wait_send()

    @pl.loop(0, 8)
    def _(k):
        n_out(k).wait_send()
        w_out(k).wait_send()


def on_device(tokens, gain, qkv_weight, out_weight, row_cells, upstream):
    queries = (BAND_ROWS, QUERY_COLS, 128)
    keys = (KEY_ROWS, KEY_COLS, 128)
    halo = (2, REACH, LONGITUDES, 128)
    wide = (8, HALF, WIDTH)
    pairs = (8, HALF, 128)
    update, grad_input, grads = pl.pallas_call(
        sublayer_kernel,
        out_shape=(
            jax.ShapeDtypeStruct((HALF, WIDTH), F32),
            jax.ShapeDtypeStruct((HALF, WIDTH), F32),
            jax.ShapeDtypeStruct((2, 128, WIDTH), BF),
        ),
        in_specs=[pl.BlockSpec(memory_space=VMEM)] * 5 + [pl.BlockSpec(memory_space=pltpu.SMEM)],
        out_specs=[pl.BlockSpec(memory_space=VMEM)] * 3,
        scratch_shapes=[
            VMEM(keys, BF),
            VMEM((2, BAND_ROWS * TILE, 128), BF),
            VMEM((BAND_ROWS, LONGITUDES, WIDTH), BF),
            VMEM(wide, BF),
            VMEM((512, WIDTH), BF),
            VMEM((8, 128, WIDTH), BF),
            VMEM(keys, BF),
            VMEM(queries, F32),
            VMEM(queries, F32),
            VMEM(queries, F32),
            VMEM(keys, F32),
            VMEM(halo, BF),
            VMEM(halo, BF),
            VMEM((BAND_ROWS, LONGITUDES, 256), BF),
            VMEM((BAND_ROWS, HALF, 256), BF),
            VMEM(pairs, BF),
            VMEM((BAND_ROWS, LONGITUDES, 128), BF),
            VMEM(pairs, BF),
            VMEM(pairs, BF),
            VMEM(wide, BF),
            VMEM(wide, BF),
            VMEM((2, HALF, WIDTH), BF),
            VMEM((2, HALF, WIDTH), F32),
            VMEM((2, 128, WIDTH), F32),
            VMEM((2, 128, WIDTH), BF),
            VMEM((3, HEAD_WIDTH, WIDTH), F32),
            VMEM((2, 16, 16, WIDTH // 2), BF),
            VMEM((2, 128, WIDTH), BF),
        ]
        + [DMA((8,))] * 14
        + [DMA((16,))] * 2
        + [DMA((8,))] * 4
        + [DMA((16,))] * 2
        + [DMA((32,))] * 4
        + [DMA((6,))] * 2,
        compiler_params=pltpu.CompilerParams(
            collective_id=0, has_side_effects=True, vmem_limit_bytes=56 << 20
        ),
        name="sublayer",
    )(
        tokens,
        gain.reshape(1, WIDTH),
        qkv_weight.reshape(3 * HEAD_WIDTH, WIDTH),
        out_weight.reshape(HEAD_WIDTH, WIDTH),
        upstream,
        row_cells,
    )
    grads = grads.astype(F32)
    grad_qkv = jnp.concatenate([grads[0, 0:HEAD_WIDTH], grads[1]], axis=0)
    return (
        update.astype(BF),
        grad_input.astype(BF),
        grad_qkv.reshape(1, 3 * HEAD_WIDTH, WIDTH),
        grads[0, HEAD_WIDTH:].reshape(1, HEAD_WIDTH, WIDTH),
    )


def solution(mesh):
    return jax.shard_map(
        on_device,
        mesh=mesh,
        in_specs=(
            P(("lat", "mp"), None),
            P(),
            P("mp", None, None),
            P("mp", None, None),
            P(),
            P(("lat", "mp"), None),
        ),
        out_specs=(
            P(("lat", "mp"), None),
            P(("lat", "mp"), None),
            P("mp", None, None),
            P("mp", None, None),
        ),
        check_vma=False,
    )
```

```python
import math

import jax
import jax.numpy as jnp
from jax import lax
from jax.experimental import pallas as pl
from jax.experimental.pallas import tpu as pltpu
from jax.sharding import PartitionSpec as P

WIDTH = 1024
HEAD_WIDTH = 64
LONGITUDES = 256
BAND_ROWS = 8
REACH = 6
KEY_ROWS = BAND_ROWS + 2 * REACH
TILE = 16
WINDOW = 2 * TILE
TILES = LONGITUDES // TILE
KEY_COLS = LONGITUDES + TILE
QUERY_COLS = LONGITUDES + TILE // 2
NEVER = -1e30
VMEM = pltpu.VMEM
MESH = pl.DeviceIdType.MESH
HALF = LONGITUDES // 2
BF = jnp.bfloat16
F32 = jnp.float32
DMA = pltpu.SemaphoreType.DMA


def row_features(row, cells):
    shape = (KEY_COLS, 128)
    col = lax.broadcasted_iota(jnp.int32, shape, 0)
    lane = lax.broadcasted_iota(jnp.int32, shape, 1)
    live = (col & (LONGITUDES - 1)) < cells
    near_row = (row >= lane - 8) & (row <= lane - 8 + 2 * REACH)
    apart = (col - lane) & 31
    near_col = (apart <= REACH) | (apart >= 32 - REACH)
    barred = (
        ((lane == 0) & ~live)
        | ((lane >= 8) & (lane < 16) & ~near_row)
        | ((lane >= 32) & (lane < 64) & ~near_col)
    )
    return jnp.where(barred, NEVER, 0.0).astype(BF)


def query_features(parity):
    shape = (BAND_ROWS, TILE, 128)
    row, col, lane = (lax.broadcasted_iota(jnp.int32, shape, d) for d in range(3))
    picked = (
        (lane == 0)
        | (lane == 8 + row)
        | (lane == 32 + ((TILE * parity + TILE // 2 + col) & 31))
    )
    return jnp.where(picked, 1.0, 0.0).reshape(BAND_ROWS * TILE, 128).astype(BF)


def attention_tile(i, kv_ref, feat_ref, q_ref, g_ref, pick_ref, cells, oq_ref, dkv_ref):
    queries = BAND_ROWS * TILE
    keys = KEY_ROWS * WINDOW
    c0 = pl.multiple_of(i * TILE, TILE)
    at = pl.multiple_of(i * TILE + TILE // 2, TILE // 2)
    kv = kv_ref[:, pl.ds(c0, WINDOW), :].reshape(keys, 128)
    feat = feat_ref[:, pl.ds(c0, WINDOW), :].reshape(keys, 128)
    q = q_ref[:, pl.ds(at, TILE), :].reshape(queries, 128).astype(jnp.bfloat16)
    g = g_ref[:, pl.ds(at, TILE), :].reshape(queries, 128).astype(jnp.bfloat16)
    pick = pick_ref[lax.rem(i, 2)]
    both = jnp.concatenate(
        [
            jnp.concatenate([q, pick], axis=1),
            jnp.concatenate([g, jnp.zeros_like(g)], axis=1),
        ],
        axis=0,
    )
    products = lax.dot_general(
        jnp.concatenate([kv, feat], axis=1),
        both,
        (((1,), (1,)), ((), ())),
        preferred_element_type=jnp.float32,
    )
    scores = products[:, :queries]
    grad_probs = products[:, queries:]
    highest = jnp.max(scores, axis=0, keepdims=True)
    terms = jnp.exp(scores - highest)
    query = lax.broadcasted_iota(jnp.int32, (1, queries), 1)
    col = (i * TILE + TILE // 2 + (query & (TILE - 1))) & (LONGITUDES - 1)
    live = jnp.where(col < cells, 1.0, 0.0)
    probs = terms * (live / jnp.sum(terms, axis=0, keepdims=True))
    weights = probs.astype(jnp.bfloat16)
    row_delta = jnp.sum(probs * grad_probs, axis=0, keepdims=True)
    grad_scores = (probs * (grad_probs - row_delta)).astype(jnp.bfloat16)
    pair = jnp.concatenate([weights, grad_scores], axis=1)
    dkv = jnp.dot(pair, jnp.concatenate([g, q], axis=0), preferred_element_type=jnp.float32)
    dkv_ref[:, pl.ds(c0, WINDOW), :] += dkv.reshape(KEY_ROWS, WINDOW, 128)
    out = lax.dot_general(
        pair, kv, (((0,), (0,)), ((), ())), preferred_element_type=jnp.float32
    )
    lane = lax.broadcasted_iota(jnp.int32, (queries, 128), 1)
    oq = jnp.where(lane < HEAD_WIDTH, out[queries:] * (1.0 / math.sqrt(HEAD_WIDTH)), out[:queries])
    oq_ref[:, pl.ds(at, TILE), :] = oq.reshape(BAND_ROWS, TILE, 128)


def remote(src, dst, send_sem, recv_sem, device):
    return pltpu.make_async_remote_copy(
        src_ref=src,
        dst_ref=dst,
        send_sem=send_sem,
        recv_sem=recv_sem,
        device_id=device,
        device_id_type=MESH,
    )


def sublayer_kernel(
    tok_ref, gain_ref, w_ref, wo_ref, up_ref, cells_ref,
    update_ref, grad_in_ref, grads_ref,
    feat, pick, nb, ub, wp, wall, kv, q, g, oq, dkv, hs, hr, ab, asib, ds, gb, os, oa, gs, gr, gy, mine, wg, wgb, wx, lr, lf,
    sn, rn, snf, rnf, su, ru, sw, rw, swf, rwf, sku, rku, skd, rkd, shg, rhg, so, ro, sgn, rgn,
    sd, rd, sl, rl, sf, rf, sp, rp, ring,
):
    lat, mp = lax.axis_index("lat"), lax.axis_index("mp")
    y, x, core = mp // 8, (mp // 2) % 4, mp % 2
    me = mp // 2
    across = (1 - y) * 4 + x
    sibling = {"mp": me * 2 + (1 - core)}

    def halves(width):
        return (
            pl.ds(pl.multiple_of(core * width, width), width),
            pl.ds(pl.multiple_of((1 - core) * width, width), width),
        )

    own_half, other_half = halves(HALF)
    own_head, other_head = halves(HEAD_WIDTH)

    def chip(k):
        d = k % 4
        d = d + (d // 2) * (1 - 2 * (d % 2))
        return ((y + k // 4) % 2) * 4 + (x + d) % 4

    def peer(row):
        return {"mp": row * 2 + core}

    def along(step):
        return {"lat": (lat + step) % 16}

    barrier = pltpu.get_barrier_semaphore()

    for device in (peer(across), peer(chip(1)), peer(chip(2)), sibling, along(1), along(15)):
        pl.semaphore_signal(barrier, inc=1, device_id=device, device_id_type=MESH)

    def tell(i):
        for step in (2**i, 16 - 2**i):
            pl.semaphore_signal(ring.at[i], inc=1, device_id=along(step), device_id_type=MESH)

    def normalised():
        features = tok_ref[...].astype(F32)
        inverse = lax.rsqrt(jnp.mean(features * features, axis=1, keepdims=True) + 1e-06)
        return features, inverse

    features, inverse = normalised()
    nb[me, own_half, :] = (features * inverse * gain_ref[...]).astype(BF)
    ub[me] = up_ref[...]
    wall[me, own_head, :] = wo_ref[...]
    wp[0:64, :] = w_ref[0:64, :]
    wp[64:128, :] = jnp.zeros((64, WIDTH), BF)
    wp[128:256, :] = w_ref[64:192, :]
    pl.semaphore_wait(barrier, 6)

    east, west, opposite = chip(1), chip(2), chip(3)
    across_east, across_west, across_opposite = chip(5), chip(6), chip(7)

    class Gather:
        def __init__(self, buf, cut, s, r):
            self.at = lambda row: buf.at[row] if cut is None else buf.at[row, cut]
            self.s, self.r = s, r

        def move(self, i):
            block = (me, me, me, across, across, west, across_east)[i]
            to = (across, east, west, east, west, east, west)[i]
            return remote(self.at(block), self.at(block), self.s.at[i], self.r.at[block], peer(to))

        def arrive(self, row):
            remote(self.at(row), self.at(row), self.s.at[0], self.r.at[row], peer(row)).wait_recv()

    def handing(buf, cut, cut_in, s, r):
        def out(row):
            return remote(buf.at[row, cut], buf.at[row, cut], s.at[row], r.at[row], sibling)

        def into(row):
            return remote(buf.at[row, cut_in], buf.at[row, cut_in], s.at[row], r.at[row], sibling)

        return out, into

    n_gather = Gather(nb, own_half, sn, rn)
    n_out, n_in = handing(nb, own_half, other_half, snf, rnf)
    w_gather = Gather(wall, own_head, sw, rw)
    w_out, w_in = handing(wall, own_head, other_head, swf, rwf)
    u_gather = Gather(ub, None, su, ru)

    for i in range(3):
        n_gather.move(i).start()
    n_out(me).start()
    for i in range(3):
        w_gather.move(i).start()
    w_out(me).start()
    weights_over = remote(wp.at[0:256], wp.at[256:512], sp.at[0], rp.at[0], sibling)
    weights_over.start()

    def cells_of(row):
        inside = (row >= 0) & (row < 128)
        return jnp.where(inside, cells_ref[jnp.clip(row, 0, 127)], 0)

    tell(0)
    dkv[...] = jnp.zeros_like(dkv)

    @pl.loop(0, KEY_ROWS)
    def _(row):
        feat[row] = row_features(row, cells_of(lat * BAND_ROWS + row - REACH))

    pick[0] = query_features(0)
    pick[1] = query_features(1)
    query_row = lax.broadcasted_iota(jnp.int32, (1, BAND_ROWS * TILE), 1) // TILE
    query_cells = jnp.zeros((1, BAND_ROWS * TILE), jnp.int32)
    for r in range(BAND_ROWS):
        query_cells = jnp.where(query_row == r, cells_of(lat * BAND_ROWS + r), query_cells)

    def whole(row):
        return kv.at[row, 0:LONGITUDES]

    def up_halo(row):
        return remote(whole(REACH + row), whole(row + REACH - BAND_ROWS), sku.at[row], rku.at[row], along(1))

    def down_halo(row):
        return remote(whole(REACH + row), whole(row + REACH + BAND_ROWS), skd.at[row], rkd.at[row], along(15))

    def project(row):
        n_in(row).wait_recv()
        made = lax.dot_general(
            nb[row], wp[0:256, :], (((1,), (1,)), ((), ())), preferred_element_type=F32
        ).astype(BF)
        kv[REACH + row, 0:LONGITUDES, :] = made[:, 128:256]
        kv[REACH + row, LONGITUDES:KEY_COLS, :] = made[0:TILE, 128:256]

        @pl.when(row >= BAND_ROWS - REACH)
        def _():
            up_halo(row).start()

        @pl.when(row < REACH)
        def _():
            down_halo(row).start()

        scaled = made[:, 0:128].astype(F32) * (1.0 / math.sqrt(HEAD_WIDTH))
        q[row, 0:LONGITUDES, :] = scaled
        q[row, LONGITUDES:QUERY_COLS, :] = scaled[0 : TILE // 2]

    def passed_on(gather, out, row, moves):
        gather.arrive(row)
        for i in moves:
            gather.move(i).start()
        out(row).start()

    def cotangent(row, c):
        k = row * 2 + c
        return remote(ds.at[row], gb.at[me, own_half], sd.at[k], rd.at[mp], {"mp": k})

    def cotangent_in(row, c):
        cut = pl.ds(c * HALF, HALF)
        k = row * 2 + c
        return remote(gb.at[row, cut], gb.at[row, cut], sd.at[k], rd.at[k], {"mp": k})

    def cotangents(row):
        w_in(row).wait_recv()
        ds[row] = lax.dot_general(
            up_ref[...], wall[row], (((1,), (1,)), ((), ())), preferred_element_type=F32
        ).astype(BF)
        cotangent(row, 0).start()
        cotangent(row, 1).start()

    project(me)
    passed_on(n_gather, n_out, west, (5,))
    passed_on(n_gather, n_out, across, (3, 4))
    passed_on(w_gather, w_out, west, (5,))
    passed_on(w_gather, w_out, across, (3, 4))
    passed_on(n_gather, n_out, east, ())
    project(west)
    project(across)
    pl.semaphore_wait(ring.at[0], 2)
    tell(1)
    passed_on(n_gather, n_out, across_east, (6,))
    passed_on(w_gather, w_out, across_east, (6,))
    project(east)
    passed_on(n_gather, n_out, opposite, ())
    project(across_east)
    passed_on(n_gather, n_out, across_west, ())
    project(opposite)
    passed_on(w_gather, w_out, east, ())
    passed_on(w_gather, w_out, across_west, ())
    cotangents(west)
    cotangents(across)
    cotangents(across_east)
    passed_on(n_gather, n_out, across_opposite, ())
    project(across_west)
    passed_on(w_gather, w_out, opposite, ())
    passed_on(w_gather, w_out, across_opposite, ())
    cotangents(east)
    cotangents(across_west)
    cotangents(opposite)
    project(across_opposite)
    cotangents(across_opposite)
    w_in(me).wait_recv()
    ds[me] = lax.dot_general(
        up_ref[...], wall[me], (((1,), (1,)), ((), ())), preferred_element_type=F32
    ).astype(BF)
    home = remote(ds.at[me], gb.at[me, own_half], sp.at[5], rp.at[5], sibling)
    home.start()
    gb[me, own_half, :] = ds[me]
    for i in range(3):
        u_gather.move(i).start()

    lane = lax.broadcasted_iota(jnp.int32, (LONGITUDES, 128), 1)

    def cotangent_rows(row):
        pair = gb[row].astype(F32)
        pair = jnp.where(core == 0, pltpu.roll(pair, HEAD_WIDTH, 1), pair)
        pair = jnp.where(lane < HEAD_WIDTH, 0.0, pair)
        g[row, 0:LONGITUDES, :] = pair
        g[row, LONGITUDES:QUERY_COLS, :] = pair[0 : TILE // 2]

    @pl.loop(1, 8)
    def _(k):
        cotangent_in(chip(k), 0).wait_recv()
        cotangent_in(chip(k), 1).wait_recv()
        cotangent_rows(chip(k))

    home.wait()
    cotangent_rows(me)

    @pl.loop(0, REACH)
    def _(row):
        up_halo(row + BAND_ROWS - REACH).wait()
        down_halo(row).wait()

    kv[0:REACH, LONGITUDES:KEY_COLS, :] = kv[0:REACH, 0:TILE, :]
    kv[BAND_ROWS + REACH : KEY_ROWS, LONGITUDES:KEY_COLS, :] = kv[BAND_ROWS + REACH : KEY_ROWS, 0:TILE, :]

    pl.semaphore_wait(ring.at[1], 2)
    tell(2)

    def halo_cut(j):
        return pl.ds(pl.multiple_of(j * WINDOW, WINDOW), WINDOW)

    def down_grad(j):
        cut = halo_cut(j)
        return remote(hs.at[0, :, cut], hr.at[0, :, cut], shg.at[j], rhg.at[j], along(15))

    def up_grad(j):
        cut = halo_cut(j)
        return remote(hs.at[1, :, cut], hr.at[1, :, cut], shg.at[j + 8], rhg.at[j + 8], along(1))

    def leave(j):
        cut = pl.ds(pl.multiple_of(j * WINDOW + TILE, TILE), WINDOW)
        hs[0, :, halo_cut(j), :] = dkv[0:REACH, cut, :].astype(BF)
        hs[1, :, halo_cut(j), :] = dkv[BAND_ROWS + REACH : KEY_ROWS, cut, :].astype(BF)
        down_grad(j).start()
        up_grad(j).start()

    @pl.loop(0, TILES)
    def _(i):
        attention_tile(i, kv, feat, q, g, pick, query_cells, oq, dkv)

        @pl.when((i % 2 == 0) & (i > 0))
        def _():
            leave(i // 2 - 1)

        @pl.when(i == 6)
        def _():
            u_gather.arrive(across)
            u_gather.move(3).start()
            u_gather.move(4).start()

        @pl.when(i == 8)
        def _():
            u_gather.arrive(west)
            u_gather.move(5).start()

        @pl.when(i == 13)
        def _():
            u_gather.arrive(across_east)
            u_gather.move(6).start()

    dkv[:, LONGITUDES:KEY_COLS, :] += dkv[:, :TILE, :]
    leave(7)
    half = TILE // 2
    oq[:, :half, :] = oq[:, LONGITUDES : LONGITUDES + half, :]
    ab[:, :, 0:128] = oq[:, 0:LONGITUDES, :].astype(BF)
    oq_over = remote(ab.at[:, other_half, 0:128], asib.at[:, :, 0:128], sp.at[1], rp.at[1], sibling)
    oq_over.start()

    columns = 512

    @pl.loop(0, WIDTH // columns)
    def _(n):
        cut = pl.ds(pl.multiple_of(n * columns, columns), columns)
        part = lax.dot_general(
            ab[:, :, 0:128].reshape(BAND_ROWS * LONGITUDES, 128),
            nb[:, :, cut].reshape(BAND_ROWS * LONGITUDES, columns),
            (((0,), (0,)), ((), ())),
            preferred_element_type=F32,
        )
        wg[0, 0:64, cut] = part[0:64]

    weights_over.wait()
    oq_over.wait()

    low = lax.broadcasted_iota(jnp.int32, (HALF, 128), 1) < HEAD_WIDTH

    @pl.loop(0, BAND_ROWS)
    def _(row):
        ours = ab[row, own_half, 0:128].astype(F32)
        theirs = asib[row, :, 0:128].astype(F32)
        first = jnp.where(core == 0, ours, theirs)
        second = jnp.where(core == 0, theirs, ours)
        os[row] = jnp.where(low, pltpu.roll(first, HEAD_WIDTH, 1), second).astype(BF)

    def heads_sent(k):
        return remote(os.at[chip(k)], oa.at[me], so.at[k], ro.at[me], peer(chip(k)))

    def heads_received(row):
        return remote(oa.at[row], oa.at[row], so.at[0], ro.at[row], peer(row))

    @pl.loop(1, 8)
    def _(k):
        heads_sent(k).start()

    oa[me] = os[me]

    for row in (east, across_west, opposite, across_opposite):
        u_gather.arrive(row)

    @pl.loop(0, WIDTH // columns)
    def _(n):
        cut = pl.ds(pl.multiple_of(n * columns, columns), columns)
        part = lax.dot_general(
            os[...].reshape(BAND_ROWS * HALF, 128),
            ub[:, :, cut].reshape(BAND_ROWS * HALF, columns),
            (((0,), (0,)), ((), ())),
            preferred_element_type=F32,
        )
        wx[0:2, :, cut] = part.reshape(2, HEAD_WIDTH, columns)

    out_over = remote(wx.at[1 - core], wx.at[2], sp.at[3], rp.at[3], sibling)
    out_over.start()

    @pl.loop(0, 8)
    def _(j):
        down_grad(j).wait()
        up_grad(j).wait()

    dkv[BAND_ROWS : BAND_ROWS + REACH, TILE:KEY_COLS, :] += hr[0].astype(F32)
    dkv[REACH : 2 * REACH, TILE:KEY_COLS, :] += hr[1].astype(F32)
    ab[:, TILE:LONGITUDES, 128:256] = dkv[REACH : REACH + BAND_ROWS, TILE:LONGITUDES, :].astype(BF)
    ab[:, 0:TILE, 128:256] = dkv[REACH : REACH + BAND_ROWS, LONGITUDES:KEY_COLS, :].astype(BF)
    kv_over = remote(ab.at[:, other_half, 128:256], asib.at[:, :, 128:256], sp.at[2], rp.at[2], sibling)
    kv_over.start()

    def share(b):
        rows = pl.ds(pl.multiple_of((b // 2) * 16, 16), 16)
        return rows, pl.ds(pl.multiple_of((b % 2) * columns, columns), columns)

    def scatter(p, k):
        rows, cut = share((lat + k) % 16)
        return remote(wgb.at[p, rows, cut], lr.at[p, k], sl.at[p * 16 + k], rl.at[p * 16 + k], along(k))

    def gather(p, k):
        rows, cut = share(lat)
        return remote(lf.at[p, rows, cut], lf.at[p, rows, cut], sf.at[p * 16 + k], rf.at[p * 16 + k], along(k))

    def gathered(p, k):
        rows, cut = share((lat + 16 - k) % 16)
        return remote(lf.at[p, rows, cut], lf.at[p, rows, cut], sf.at[p * 16 + k], rf.at[p * 16 + k], along(k))

    def scatter_all(p):
        wgb[p] = wg[p].astype(BF)

        @pl.loop(1, 16)
        def _(k):
            scatter(p, k).start()

    def sum_all(p):
        rows, cut = share(lat)
        total = wg[p, rows, cut]
        for k in range(1, 16):
            scatter(p, k).wait()
            total = total + lr[p, k].astype(F32)
        lf[p, rows, cut] = (total * (4.0 / math.sqrt(BAND_ROWS * LONGITUDES * 16))).astype(BF)

        @pl.loop(1, 16)
        def _(k):
            gather(p, k).start()

    out_over.wait()
    wg[0, 64:128, :] = wx[core] + wx[2]
    pl.semaphore_wait(ring.at[2], 2)
    scatter_all(0)
    kv_over.wait()

    def grad_part(row):
        both = jnp.concatenate([ab[row, own_half, :], asib[row]], axis=1)
        return jnp.dot(both, wp[...], preferred_element_type=F32)

    def grad_sent(i):
        to = (east, west, west, east, east, west)[i]
        return remote(gs.at[i], gr.at[i], sgn.at[i], rgn.at[i], peer(to))

    gs[1] = grad_part(across_opposite).astype(BF)
    grad_sent(1).start()
    gs[0] = grad_part(opposite).astype(BF)
    grad_sent(0).start()
    gs[3] = grad_part(across_east).astype(BF)
    grad_sent(3).start()

    @pl.loop(0, WIDTH // columns)
    def _(n):
        cut = pl.ds(pl.multiple_of(n * columns, columns), columns)
        wg[1, :, cut] = lax.dot_general(
            ab[:, :, 128:256].reshape(BAND_ROWS * LONGITUDES, 128),
            nb[:, :, cut].reshape(BAND_ROWS * LONGITUDES, columns),
            (((0,), (0,)), ((), ())),
            preferred_element_type=F32,
        )

    scatter_all(1)
    mine[1] = grad_part(across_west)
    grad_sent(1).wait_recv()
    gs[2] = (mine[1] + gr[1].astype(F32)).astype(BF)
    grad_sent(2).start()
    mine[0] = grad_part(east)
    grad_sent(0).wait_recv()
    gs[4] = (mine[0] + gr[0].astype(F32)).astype(BF)
    grad_sent(4).start()
    gs[5] = grad_part(west).astype(BF)
    grad_sent(5).start()
    mine[0] = grad_part(me)
    mine[1] = grad_part(across)
    sum_all(0)
    grad_sent(2).wait_recv()
    grad_sent(3).wait_recv()
    gy[0] = (mine[1] + gr[2].astype(F32) + gr[3].astype(F32)).astype(BF)
    over_y = remote(gy.at[0], gy.at[1], sp.at[4], rp.at[4], peer(across))
    over_y.start()
    sum_all(1)

    @pl.loop(1, 8)
    def _(k):
        heads_received(chip(k)).wait_recv()

    heads = jnp.concatenate([oa[k] for k in range(8)], axis=1)
    update_ref[...] = jnp.dot(heads, wall[...].reshape(WIDTH, WIDTH), preferred_element_type=F32)

    grad_sent(4).wait_recv()
    grad_sent(5).wait_recv()
    total = mine[0] + gr[4].astype(F32) + gr[5].astype(F32)
    over_y.wait()
    total = total + gy[1].astype(F32)
    features, inverse = normalised()
    centred = features * inverse
    scaled = gain_ref[...] * total
    grad_in_ref[...] = inverse * (
        scaled - centred * jnp.mean(scaled * centred, axis=1, keepdims=True)
    )

    @pl.loop(1, 16)
    def _(k):
        for p in range(2):
            gather(p, k).wait_send()
            gathered(p, k).wait_recv()

    @pl.loop(1, 8)
    def _(k):
        cotangent(chip(k), 0).wait_send()
        cotangent(chip(k), 1).wait_send()

    grads_ref[...] = lf[...]

    for i in range(7):
        n_gather.move(i).wait_send()
        w_gather.move(i).wait_send()
        u_gather.move(i).wait_send()
    for i in range(6):
        grad_sent(i).wait_send()

    @pl.loop(1, 8)
    def _(k):
        heads_sent(k).wait_send()

    @pl.loop(0, 8)
    def _(k):
        n_out(k).wait_send()
        w_out(k).wait_send()


def on_device(tokens, gain, qkv_weight, out_weight, row_cells, upstream):
    queries = (BAND_ROWS, QUERY_COLS, 128)
    keys = (KEY_ROWS, KEY_COLS, 128)
    halo = (2, REACH, LONGITUDES, 128)
    wide = (8, HALF, WIDTH)
    pairs = (8, HALF, 128)
    update, grad_input, grads = pl.pallas_call(
        sublayer_kernel,
        out_shape=(
            jax.ShapeDtypeStruct((HALF, WIDTH), F32),
            jax.ShapeDtypeStruct((HALF, WIDTH), F32),
            jax.ShapeDtypeStruct((2, 128, WIDTH), BF),
        ),
        in_specs=[pl.BlockSpec(memory_space=VMEM)] * 5 + [pl.BlockSpec(memory_space=pltpu.SMEM)],
        out_specs=[pl.BlockSpec(memory_space=VMEM)] * 3,
        scratch_shapes=[
            VMEM(keys, BF),
            VMEM((2, BAND_ROWS * TILE, 128), BF),
            VMEM((BAND_ROWS, LONGITUDES, WIDTH), BF),
            VMEM(wide, BF),
            VMEM((512, WIDTH), BF),
            VMEM((8, 128, WIDTH), BF),
            VMEM(keys, BF),
            VMEM(queries, F32),
            VMEM(queries, F32),
            VMEM(queries, F32),
            VMEM(keys, F32),
            VMEM(halo, BF),
            VMEM(halo, BF),
            VMEM((BAND_ROWS, LONGITUDES, 256), BF),
            VMEM((BAND_ROWS, HALF, 256), BF),
            VMEM(pairs, BF),
            VMEM((BAND_ROWS, LONGITUDES, 128), BF),
            VMEM(pairs, BF),
            VMEM(pairs, BF),
            VMEM(wide, BF),
            VMEM(wide, BF),
            VMEM((2, HALF, WIDTH), BF),
            VMEM((2, HALF, WIDTH), F32),
            VMEM((2, 128, WIDTH), F32),
            VMEM((2, 128, WIDTH), BF),
            VMEM((3, HEAD_WIDTH, WIDTH), F32),
            VMEM((2, 16, 16, WIDTH // 2), BF),
            VMEM((2, 128, WIDTH), BF),
        ]
        + [DMA((8,))] * 14
        + [DMA((16,))] * 2
        + [DMA((8,))] * 4
        + [DMA((16,))] * 2
        + [DMA((32,))] * 4
        + [DMA((6,))] * 2
        + [pltpu.SemaphoreType.REGULAR((3,))],
        compiler_params=pltpu.CompilerParams(
            collective_id=0, has_side_effects=True, vmem_limit_bytes=56 << 20
        ),
        name="sublayer",
    )(
        tokens,
        gain.reshape(1, WIDTH),
        qkv_weight.reshape(3 * HEAD_WIDTH, WIDTH),
        out_weight.reshape(HEAD_WIDTH, WIDTH),
        upstream,
        row_cells,
    )
    grads = grads.astype(F32)
    grad_qkv = jnp.concatenate([grads[0, 0:HEAD_WIDTH], grads[1]], axis=0)
    return (
        update.astype(BF),
        grad_input.astype(BF),
        grad_qkv.reshape(1, 3 * HEAD_WIDTH, WIDTH),
        grads[0, HEAD_WIDTH:].reshape(1, HEAD_WIDTH, WIDTH),
    )


def solution(mesh):
    return jax.shard_map(
        on_device,
        mesh=mesh,
        in_specs=(
            P(("lat", "mp"), None),
            P(),
            P("mp", None, None),
            P("mp", None, None),
            P(),
            P(("lat", "mp"), None),
        ),
        out_specs=(
            P(("lat", "mp"), None),
            P(("lat", "mp"), None),
            P("mp", None, None),
            P("mp", None, None),
        ),
        check_vma=False,
    )
```

```python
import math

import jax
import jax.numpy as jnp
from jax import lax
from jax.experimental import pallas as pl
from jax.experimental.pallas import tpu as pltpu
from jax.sharding import PartitionSpec as P

WIDTH = 1024
HEAD_WIDTH = 64
LONGITUDES = 256
BAND_ROWS = 8
REACH = 6
KEY_ROWS = BAND_ROWS + 2 * REACH
TILE = 16
WINDOW = 2 * TILE
TILES = LONGITUDES // TILE
KEY_COLS = LONGITUDES + TILE
QUERY_COLS = LONGITUDES + TILE // 2
NEVER = -1e30
VMEM = pltpu.VMEM
MESH = pl.DeviceIdType.MESH
HALF = LONGITUDES // 2
BF = jnp.bfloat16
F32 = jnp.float32
DMA = pltpu.SemaphoreType.DMA


def row_features(row, cells):
    shape = (KEY_COLS, 128)
    col = lax.broadcasted_iota(jnp.int32, shape, 0)
    lane = lax.broadcasted_iota(jnp.int32, shape, 1)
    live = (col & (LONGITUDES - 1)) < cells
    near_row = (row >= lane - 8) & (row <= lane - 8 + 2 * REACH)
    apart = (col - lane) & 31
    near_col = (apart <= REACH) | (apart >= 32 - REACH)
    barred = (
        ((lane == 0) & ~live)
        | ((lane >= 8) & (lane < 16) & ~near_row)
        | ((lane >= 32) & (lane < 64) & ~near_col)
    )
    return jnp.where(barred, NEVER, 0.0).astype(BF)


def query_features(parity):
    shape = (BAND_ROWS, TILE, 128)
    row, col, lane = (lax.broadcasted_iota(jnp.int32, shape, d) for d in range(3))
    picked = (
        (lane == 0)
        | (lane == 8 + row)
        | (lane == 32 + ((TILE * parity + TILE // 2 + col) & 31))
    )
    return jnp.where(picked, 1.0, 0.0).reshape(BAND_ROWS * TILE, 128).astype(BF)


def attention_tile(i, kv_ref, feat_ref, q_ref, g_ref, pick_ref, cells, oq_ref, dkv_ref):
    queries = BAND_ROWS * TILE
    keys = KEY_ROWS * WINDOW
    c0 = pl.multiple_of(i * TILE, TILE)
    at = pl.multiple_of(i * TILE + TILE // 2, TILE // 2)
    kv = kv_ref[:, pl.ds(c0, WINDOW), :].reshape(keys, 128)
    feat = feat_ref[:, pl.ds(c0, WINDOW), :].reshape(keys, 128)
    q = q_ref[:, pl.ds(at, TILE), :].reshape(queries, 128).astype(jnp.bfloat16)
    g = g_ref[:, pl.ds(at, TILE), :].reshape(queries, 128).astype(jnp.bfloat16)
    pick = pick_ref[lax.rem(i, 2)]
    both = jnp.concatenate(
        [
            jnp.concatenate([q, pick], axis=1),
            jnp.concatenate([g, jnp.zeros_like(g)], axis=1),
        ],
        axis=0,
    )
    products = lax.dot_general(
        jnp.concatenate([kv, feat], axis=1),
        both,
        (((1,), (1,)), ((), ())),
        preferred_element_type=jnp.float32,
    )
    scores = products[:, :queries]
    grad_probs = products[:, queries:]
    highest = jnp.max(scores, axis=0, keepdims=True)
    terms = jnp.exp(scores - highest)
    query = lax.broadcasted_iota(jnp.int32, (1, queries), 1)
    col = (i * TILE + TILE // 2 + (query & (TILE - 1))) & (LONGITUDES - 1)
    live = jnp.where(col < cells, 1.0, 0.0)
    probs = terms * (live / jnp.sum(terms, axis=0, keepdims=True))
    weights = probs.astype(jnp.bfloat16)
    row_delta = jnp.sum(probs * grad_probs, axis=0, keepdims=True)
    grad_scores = (probs * (grad_probs - row_delta)).astype(jnp.bfloat16)
    pair = jnp.concatenate([weights, grad_scores], axis=1)
    dkv = jnp.dot(pair, jnp.concatenate([g, q], axis=0), preferred_element_type=jnp.float32)
    dkv_ref[:, pl.ds(c0, WINDOW), :] += dkv.reshape(KEY_ROWS, WINDOW, 128)
    out = lax.dot_general(
        pair, kv, (((0,), (0,)), ((), ())), preferred_element_type=jnp.float32
    )
    lane = lax.broadcasted_iota(jnp.int32, (queries, 128), 1)
    oq = jnp.where(lane < HEAD_WIDTH, out[queries:] * (1.0 / math.sqrt(HEAD_WIDTH)), out[:queries])
    oq_ref[:, pl.ds(at, TILE), :] = oq.reshape(BAND_ROWS, TILE, 128)


def remote(src, dst, send_sem, recv_sem, device):
    return pltpu.make_async_remote_copy(
        src_ref=src,
        dst_ref=dst,
        send_sem=send_sem,
        recv_sem=recv_sem,
        device_id=device,
        device_id_type=MESH,
    )


def sublayer_kernel(
    tok_ref, gain_ref, w_ref, wo_ref, up_ref, cells_ref,
    update_ref, grad_in_ref, grads_ref,
    feat, pick, nb, ub, wp, wall, kv, q, g, oq, dkv, hs, hr, ab, asib, ds, gb, os, oa, gs, gr, gy, mine, wg, wgb, wx, lr, lf,
    sn, rn, snf, rnf, su, ru, sw, rw, swf, rwf, sku, rku, skd, rkd, shg, rhg, so, ro, sgn, rgn,
    sd, rd, sl, rl, sf, rf, sp, rp, ring,
):
    lat, mp = lax.axis_index("lat"), lax.axis_index("mp")
    y, x, core = mp // 8, (mp // 2) % 4, mp % 2
    me = mp // 2
    across = (1 - y) * 4 + x
    sibling = {"mp": me * 2 + (1 - core)}

    def halves(width):
        return (
            pl.ds(pl.multiple_of(core * width, width), width),
            pl.ds(pl.multiple_of((1 - core) * width, width), width),
        )

    own_half, other_half = halves(HALF)
    own_head, other_head = halves(HEAD_WIDTH)

    def chip(k):
        d = k % 4
        d = d + (d // 2) * (1 - 2 * (d % 2))
        return ((y + k // 4) % 2) * 4 + (x + d) % 4

    def peer(row):
        return {"mp": row * 2 + core}

    def along(step):
        return {"lat": (lat + step) % 16}

    barrier = pltpu.get_barrier_semaphore()

    for device in (peer(across), peer(chip(1)), peer(chip(2)), sibling, along(1), along(15)):
        pl.semaphore_signal(barrier, inc=1, device_id=device, device_id_type=MESH)

    def tell(i):
        for step in (2**i, 16 - 2**i):
            pl.semaphore_signal(ring.at[i], inc=1, device_id=along(step), device_id_type=MESH)

    def normalised():
        features = tok_ref[...].astype(F32)
        inverse = lax.rsqrt(jnp.mean(features * features, axis=1, keepdims=True) + 1e-06)
        return features, inverse

    features, inverse = normalised()
    nb[me, own_half, :] = (features * inverse * gain_ref[...]).astype(BF)
    ub[me] = up_ref[...]
    wall[me, own_head, :] = wo_ref[...]
    wp[0:64, :] = w_ref[0:64, :]
    wp[64:128, :] = jnp.zeros((64, WIDTH), BF)
    wp[128:256, :] = w_ref[64:192, :]
    pl.semaphore_wait(barrier, 6)

    east, west, opposite = chip(1), chip(2), chip(3)
    across_east, across_west, across_opposite = chip(5), chip(6), chip(7)

    class Gather:
        def __init__(self, buf, cut, s, r):
            self.at = lambda row: buf.at[row] if cut is None else buf.at[row, cut]
            self.s, self.r = s, r

        def move(self, i):
            block = (me, me, me, across, across, west, across_east)[i]
            to = (across, east, west, east, west, east, west)[i]
            return remote(self.at(block), self.at(block), self.s.at[i], self.r.at[block], peer(to))

        def arrive(self, row):
            remote(self.at(row), self.at(row), self.s.at[0], self.r.at[row], peer(row)).wait_recv()

    def handing(buf, cut, cut_in, s, r):
        def out(row):
            return remote(buf.at[row, cut], buf.at[row, cut], s.at[row], r.at[row], sibling)

        def into(row):
            return remote(buf.at[row, cut_in], buf.at[row, cut_in], s.at[row], r.at[row], sibling)

        return out, into

    n_gather = Gather(nb, own_half, sn, rn)
    n_out, n_in = handing(nb, own_half, other_half, snf, rnf)
    w_gather = Gather(wall, own_head, sw, rw)
    w_out, w_in = handing(wall, own_head, other_head, swf, rwf)
    u_gather = Gather(ub, None, su, ru)

    for i in range(3):
        n_gather.move(i).start()
    n_out(me).start()
    for i in range(3):
        w_gather.move(i).start()
    w_out(me).start()
    weights_over = remote(wp.at[0:256], wp.at[256:512], sp.at[0], rp.at[0], sibling)
    weights_over.start()

    def cells_of(row):
        inside = (row >= 0) & (row < 128)
        return jnp.where(inside, cells_ref[jnp.clip(row, 0, 127)], 0)

    tell(0)
    dkv[...] = jnp.zeros_like(dkv)

    @pl.loop(0, KEY_ROWS)
    def _(row):
        feat[row] = row_features(row, cells_of(lat * BAND_ROWS + row - REACH))

    pick[0] = query_features(0)
    pick[1] = query_features(1)
    query_row = lax.broadcasted_iota(jnp.int32, (1, BAND_ROWS * TILE), 1) // TILE
    query_cells = jnp.zeros((1, BAND_ROWS * TILE), jnp.int32)
    for r in range(BAND_ROWS):
        query_cells = jnp.where(query_row == r, cells_of(lat * BAND_ROWS + r), query_cells)

    def whole(row):
        return kv.at[row, 0:LONGITUDES]

    def up_halo(row):
        return remote(whole(REACH + row), whole(row + REACH - BAND_ROWS), sku.at[row], rku.at[row], along(1))

    def down_halo(row):
        return remote(whole(REACH + row), whole(row + REACH + BAND_ROWS), skd.at[row], rkd.at[row], along(15))

    def project(row):
        n_in(row).wait_recv()
        made = lax.dot_general(
            nb[row], wp[0:256, :], (((1,), (1,)), ((), ())), preferred_element_type=F32
        ).astype(BF)
        kv[REACH + row, 0:LONGITUDES, :] = made[:, 128:256]
        kv[REACH + row, LONGITUDES:KEY_COLS, :] = made[0:TILE, 128:256]

        @pl.when(row >= BAND_ROWS - REACH)
        def _():
            up_halo(row).start()

        @pl.when(row < REACH)
        def _():
            down_halo(row).start()

        scaled = made[:, 0:128].astype(F32) * (1.0 / math.sqrt(HEAD_WIDTH))
        q[row, 0:LONGITUDES, :] = scaled
        q[row, LONGITUDES:QUERY_COLS, :] = scaled[0 : TILE // 2]

    def passed_on(gather, out, row, moves):
        gather.arrive(row)
        for i in moves:
            gather.move(i).start()
        out(row).start()

    def cotangent(row, c):
        k = row * 2 + c
        return remote(ds.at[row], gb.at[me, own_half], sd.at[k], rd.at[mp], {"mp": k})

    def cotangent_in(row, c):
        cut = pl.ds(c * HALF, HALF)
        k = row * 2 + c
        return remote(gb.at[row, cut], gb.at[row, cut], sd.at[k], rd.at[k], {"mp": k})

    def cotangents(row):
        w_in(row).wait_recv()
        ds[row] = lax.dot_general(
            up_ref[...], wall[row], (((1,), (1,)), ((), ())), preferred_element_type=F32
        ).astype(BF)
        cotangent(row, 0).start()
        cotangent(row, 1).start()

    project(me)
    passed_on(n_gather, n_out, west, (5,))
    passed_on(n_gather, n_out, across, (3, 4))
    passed_on(w_gather, w_out, west, (5,))
    passed_on(w_gather, w_out, across, (3, 4))
    passed_on(n_gather, n_out, east, ())
    project(west)
    project(across)
    pl.semaphore_wait(ring.at[0], 2)
    tell(1)
    passed_on(n_gather, n_out, across_east, (6,))
    passed_on(w_gather, w_out, across_east, (6,))
    project(east)
    passed_on(n_gather, n_out, opposite, ())
    project(across_east)
    passed_on(n_gather, n_out, across_west, ())
    project(opposite)
    passed_on(w_gather, w_out, east, ())
    passed_on(w_gather, w_out, across_west, ())
    cotangents(west)
    cotangents(across)
    cotangents(across_east)
    passed_on(n_gather, n_out, across_opposite, ())
    project(across_west)
    passed_on(w_gather, w_out, opposite, ())
    passed_on(w_gather, w_out, across_opposite, ())
    cotangents(east)
    cotangents(across_west)
    cotangents(opposite)
    project(across_opposite)
    cotangents(across_opposite)
    w_in(me).wait_recv()
    ds[me] = lax.dot_general(
        up_ref[...], wall[me], (((1,), (1,)), ((), ())), preferred_element_type=F32
    ).astype(BF)
    home = remote(ds.at[me], gb.at[me, own_half], sp.at[5], rp.at[5], sibling)
    home.start()
    gb[me, own_half, :] = ds[me]
    for i in range(3):
        u_gather.move(i).start()

    lane = lax.broadcasted_iota(jnp.int32, (LONGITUDES, 128), 1)

    def cotangent_rows(row):
        pair = gb[row].astype(F32)
        pair = jnp.where(core == 0, pltpu.roll(pair, HEAD_WIDTH, 1), pair)
        pair = jnp.where(lane < HEAD_WIDTH, 0.0, pair)
        g[row, 0:LONGITUDES, :] = pair
        g[row, LONGITUDES:QUERY_COLS, :] = pair[0 : TILE // 2]

    @pl.loop(1, 8)
    def _(k):
        cotangent_in(chip(k), 0).wait_recv()
        cotangent_in(chip(k), 1).wait_recv()
        cotangent_rows(chip(k))

    home.wait()
    cotangent_rows(me)

    @pl.loop(0, REACH)
    def _(row):
        up_halo(row + BAND_ROWS - REACH).wait()
        down_halo(row).wait()

    kv[0:REACH, LONGITUDES:KEY_COLS, :] = kv[0:REACH, 0:TILE, :]
    kv[BAND_ROWS + REACH : KEY_ROWS, LONGITUDES:KEY_COLS, :] = kv[BAND_ROWS + REACH : KEY_ROWS, 0:TILE, :]

    pl.semaphore_wait(ring.at[1], 2)
    tell(2)

    def halo_cut(j):
        return pl.ds(pl.multiple_of(j * WINDOW, WINDOW), WINDOW)

    def down_grad(j):
        cut = halo_cut(j)
        return remote(hs.at[0, :, cut], hr.at[0, :, cut], shg.at[j], rhg.at[j], along(15))

    def up_grad(j):
        cut = halo_cut(j)
        return remote(hs.at[1, :, cut], hr.at[1, :, cut], shg.at[j + 8], rhg.at[j + 8], along(1))

    def leave(j):
        cut = pl.ds(pl.multiple_of(j * WINDOW + TILE, TILE), WINDOW)
        hs[0, :, halo_cut(j), :] = dkv[0:REACH, cut, :].astype(BF)
        hs[1, :, halo_cut(j), :] = dkv[BAND_ROWS + REACH : KEY_ROWS, cut, :].astype(BF)
        down_grad(j).start()
        up_grad(j).start()

    @pl.loop(0, TILES)
    def _(i):
        attention_tile(i, kv, feat, q, g, pick, query_cells, oq, dkv)

        @pl.when((i % 2 == 0) & (i > 0))
        def _():
            leave(i // 2 - 1)

        @pl.when(i == 6)
        def _():
            u_gather.arrive(across)
            u_gather.move(3).start()
            u_gather.move(4).start()

        @pl.when(i == 8)
        def _():
            u_gather.arrive(west)
            u_gather.move(5).start()

        @pl.when(i == 13)
        def _():
            u_gather.arrive(across_east)
            u_gather.move(6).start()

    dkv[:, LONGITUDES:KEY_COLS, :] += dkv[:, :TILE, :]
    leave(7)
    half = TILE // 2
    oq[:, :half, :] = oq[:, LONGITUDES : LONGITUDES + half, :]
    ab[:, :, 0:128] = oq[:, 0:LONGITUDES, :].astype(BF)
    oq_over = remote(ab.at[:, other_half, 0:128], asib.at[:, :, 0:128], sp.at[1], rp.at[1], sibling)
    oq_over.start()

    columns = 512

    @pl.loop(0, WIDTH // columns)
    def _(n):
        cut = pl.ds(pl.multiple_of(n * columns, columns), columns)
        part = lax.dot_general(
            ab[:, :, 0:128].reshape(BAND_ROWS * LONGITUDES, 128),
            nb[:, :, cut].reshape(BAND_ROWS * LONGITUDES, columns),
            (((0,), (0,)), ((), ())),
            preferred_element_type=F32,
        )
        wg[0, 0:64, cut] = part[0:64]

    weights_over.wait()
    oq_over.wait()

    low = lax.broadcasted_iota(jnp.int32, (HALF, 128), 1) < HEAD_WIDTH

    @pl.loop(0, BAND_ROWS)
    def _(row):
        ours = ab[row, own_half, 0:128].astype(F32)
        theirs = asib[row, :, 0:128].astype(F32)
        first = jnp.where(core == 0, ours, theirs)
        second = jnp.where(core == 0, theirs, ours)
        os[row] = jnp.where(low, pltpu.roll(first, HEAD_WIDTH, 1), second).astype(BF)

    def heads_sent(k):
        return remote(os.at[chip(k)], oa.at[me], so.at[k], ro.at[me], peer(chip(k)))

    def heads_received(row):
        return remote(oa.at[row], oa.at[row], so.at[0], ro.at[row], peer(row))

    @pl.loop(1, 8)
    def _(k):
        heads_sent(k).start()

    oa[me] = os[me]

    for row in (east, across_west, opposite, across_opposite):
        u_gather.arrive(row)

    @pl.loop(0, WIDTH // columns)
    def _(n):
        cut = pl.ds(pl.multiple_of(n * columns, columns), columns)
        part = lax.dot_general(
            os[...].reshape(BAND_ROWS * HALF, 128),
            ub[:, :, cut].reshape(BAND_ROWS * HALF, columns),
            (((0,), (0,)), ((), ())),
            preferred_element_type=F32,
        )
        wx[0:2, :, cut] = part.reshape(2, HEAD_WIDTH, columns)

    out_over = remote(wx.at[1 - core], wx.at[2], sp.at[3], rp.at[3], sibling)
    out_over.start()

    @pl.loop(0, 8)
    def _(j):
        down_grad(j).wait()
        up_grad(j).wait()

    dkv[BAND_ROWS : BAND_ROWS + REACH, TILE:KEY_COLS, :] += hr[0].astype(F32)
    dkv[REACH : 2 * REACH, TILE:KEY_COLS, :] += hr[1].astype(F32)
    ab[:, TILE:LONGITUDES, 128:256] = dkv[REACH : REACH + BAND_ROWS, TILE:LONGITUDES, :].astype(BF)
    ab[:, 0:TILE, 128:256] = dkv[REACH : REACH + BAND_ROWS, LONGITUDES:KEY_COLS, :].astype(BF)
    kv_over = remote(ab.at[:, other_half, 128:256], asib.at[:, :, 128:256], sp.at[2], rp.at[2], sibling)
    kv_over.start()

    def share(b):
        rows = pl.ds(pl.multiple_of((b // 2) * 16, 16), 16)
        return rows, pl.ds(pl.multiple_of((b % 2) * columns, columns), columns)

    def scatter(p, k):
        rows, cut = share((lat + k) % 16)
        return remote(wgb.at[p, rows, cut], lr.at[p, k], sl.at[p * 16 + k], rl.at[p * 16 + k], along(k))

    def gather(p, k):
        rows, cut = share(lat)
        return remote(lf.at[p, rows, cut], lf.at[p, rows, cut], sf.at[p * 16 + k], rf.at[p * 16 + k], along(k))

    def gathered(p, k):
        rows, cut = share((lat + 16 - k) % 16)
        return remote(lf.at[p, rows, cut], lf.at[p, rows, cut], sf.at[p * 16 + k], rf.at[p * 16 + k], along(k))

    def scatter_all(p):
        wgb[p] = wg[p].astype(BF)

        @pl.loop(1, 16)
        def _(k):
            scatter(p, k).start()

    def sum_all(p):
        rows, cut = share(lat)
        total = wg[p, rows, cut]
        for k in range(1, 16):
            scatter(p, k).wait()
            total = total + lr[p, k].astype(F32)
        lf[p, rows, cut] = (total * (4.0 / math.sqrt(BAND_ROWS * LONGITUDES * 16))).astype(BF)

        @pl.loop(1, 16)
        def _(k):
            gather(p, k).start()

    out_over.wait()
    wg[0, 64:128, :] = wx[core] + wx[2]
    pl.semaphore_wait(ring.at[2], 2)
    scatter_all(0)
    kv_over.wait()

    def grad_part(row):
        both = jnp.concatenate([ab[row, own_half, :], asib[row]], axis=1)
        return jnp.dot(both, wp[...], preferred_element_type=F32)

    def grad_sent(i):
        to = (east, west, west, east, east, west)[i]
        return remote(gs.at[i], gr.at[i], sgn.at[i], rgn.at[i], peer(to))

    gs[1] = grad_part(across_opposite).astype(BF)
    grad_sent(1).start()
    gs[0] = grad_part(opposite).astype(BF)
    grad_sent(0).start()
    gs[3] = grad_part(across_east).astype(BF)
    grad_sent(3).start()

    @pl.loop(0, WIDTH // columns)
    def _(n):
        cut = pl.ds(pl.multiple_of(n * columns, columns), columns)
        wg[1, :, cut] = lax.dot_general(
            ab[:, :, 128:256].reshape(BAND_ROWS * LONGITUDES, 128),
            nb[:, :, cut].reshape(BAND_ROWS * LONGITUDES, columns),
            (((0,), (0,)), ((), ())),
            preferred_element_type=F32,
        )

    scatter_all(1)
    mine[1] = grad_part(across_west)
    grad_sent(1).wait_recv()
    gs[2] = (mine[1] + gr[1].astype(F32)).astype(BF)
    grad_sent(2).start()
    sum_all(0)
    mine[0] = grad_part(east)
    grad_sent(0).wait_recv()
    gs[4] = (mine[0] + gr[0].astype(F32)).astype(BF)
    grad_sent(4).start()
    gs[5] = grad_part(west).astype(BF)
    grad_sent(5).start()
    mine[0] = grad_part(me)
    mine[1] = grad_part(across)
    grad_sent(2).wait_recv()
    grad_sent(3).wait_recv()
    gy[0] = (mine[1] + gr[2].astype(F32) + gr[3].astype(F32)).astype(BF)
    over_y = remote(gy.at[0], gy.at[1], sp.at[4], rp.at[4], peer(across))
    over_y.start()
    sum_all(1)

    @pl.loop(1, 8)
    def _(k):
        heads_received(chip(k)).wait_recv()

    heads = jnp.concatenate([oa[k] for k in range(8)], axis=1)
    update_ref[...] = jnp.dot(heads, wall[...].reshape(WIDTH, WIDTH), preferred_element_type=F32)

    grad_sent(4).wait_recv()
    grad_sent(5).wait_recv()
    total = mine[0] + gr[4].astype(F32) + gr[5].astype(F32)
    over_y.wait()
    total = total + gy[1].astype(F32)
    features, inverse = normalised()
    centred = features * inverse
    scaled = gain_ref[...] * total
    grad_in_ref[...] = inverse * (
        scaled - centred * jnp.mean(scaled * centred, axis=1, keepdims=True)
    )

    @pl.loop(1, 16)
    def _(k):
        for p in range(2):
            gather(p, k).wait_send()
            gathered(p, k).wait_recv()

    @pl.loop(1, 8)
    def _(k):
        cotangent(chip(k), 0).wait_send()
        cotangent(chip(k), 1).wait_send()

    grads_ref[...] = lf[...]

    for i in range(7):
        n_gather.move(i).wait_send()
        w_gather.move(i).wait_send()
        u_gather.move(i).wait_send()
    for i in range(6):
        grad_sent(i).wait_send()

    @pl.loop(1, 8)
    def _(k):
        heads_sent(k).wait_send()

    @pl.loop(0, 8)
    def _(k):
        n_out(k).wait_send()
        w_out(k).wait_send()


def on_device(tokens, gain, qkv_weight, out_weight, row_cells, upstream):
    queries = (BAND_ROWS, QUERY_COLS, 128)
    keys = (KEY_ROWS, KEY_COLS, 128)
    halo = (2, REACH, LONGITUDES, 128)
    wide = (8, HALF, WIDTH)
    pairs = (8, HALF, 128)
    update, grad_input, grads = pl.pallas_call(
        sublayer_kernel,
        out_shape=(
            jax.ShapeDtypeStruct((HALF, WIDTH), F32),
            jax.ShapeDtypeStruct((HALF, WIDTH), F32),
            jax.ShapeDtypeStruct((2, 128, WIDTH), BF),
        ),
        in_specs=[pl.BlockSpec(memory_space=VMEM)] * 5 + [pl.BlockSpec(memory_space=pltpu.SMEM)],
        out_specs=[pl.BlockSpec(memory_space=VMEM)] * 3,
        scratch_shapes=[
            VMEM(keys, BF),
            VMEM((2, BAND_ROWS * TILE, 128), BF),
            VMEM((BAND_ROWS, LONGITUDES, WIDTH), BF),
            VMEM(wide, BF),
            VMEM((512, WIDTH), BF),
            VMEM((8, 128, WIDTH), BF),
            VMEM(keys, BF),
            VMEM(queries, F32),
            VMEM(queries, F32),
            VMEM(queries, F32),
            VMEM(keys, F32),
            VMEM(halo, BF),
            VMEM(halo, BF),
            VMEM((BAND_ROWS, LONGITUDES, 256), BF),
            VMEM((BAND_ROWS, HALF, 256), BF),
            VMEM(pairs, BF),
            VMEM((BAND_ROWS, LONGITUDES, 128), BF),
            VMEM(pairs, BF),
            VMEM(pairs, BF),
            VMEM(wide, BF),
            VMEM(wide, BF),
            VMEM((2, HALF, WIDTH), BF),
            VMEM((2, HALF, WIDTH), F32),
            VMEM((2, 128, WIDTH), F32),
            VMEM((2, 128, WIDTH), BF),
            VMEM((3, HEAD_WIDTH, WIDTH), F32),
            VMEM((2, 16, 16, WIDTH // 2), BF),
            VMEM((2, 128, WIDTH), BF),
        ]
        + [DMA((8,))] * 14
        + [DMA((16,))] * 2
        + [DMA((8,))] * 4
        + [DMA((16,))] * 2
        + [DMA((32,))] * 4
        + [DMA((6,))] * 2
        + [pltpu.SemaphoreType.REGULAR((3,))],
        compiler_params=pltpu.CompilerParams(
            collective_id=0, has_side_effects=True, vmem_limit_bytes=56 << 20
        ),
        name="sublayer",
    )(
        tokens,
        gain.reshape(1, WIDTH),
        qkv_weight.reshape(3 * HEAD_WIDTH, WIDTH),
        out_weight.reshape(HEAD_WIDTH, WIDTH),
        upstream,
        row_cells,
    )
    grads = grads.astype(F32)
    grad_qkv = jnp.concatenate([grads[0, 0:HEAD_WIDTH], grads[1]], axis=0)
    return (
        update.astype(BF),
        grad_input.astype(BF),
        grad_qkv.reshape(1, 3 * HEAD_WIDTH, WIDTH),
        grads[0, HEAD_WIDTH:].reshape(1, HEAD_WIDTH, WIDTH),
    )


def solution(mesh):
    return jax.shard_map(
        on_device,
        mesh=mesh,
        in_specs=(
            P(("lat", "mp"), None),
            P(),
            P("mp", None, None),
            P("mp", None, None),
            P(),
            P(("lat", "mp"), None),
        ),
        out_specs=(
            P(("lat", "mp"), None),
            P(("lat", "mp"), None),
            P("mp", None, None),
            P("mp", None, None),
        ),
        check_vma=False,
    )
```
